256 devices in a mesh: dp: 32 (over x, z), fsdp: 8 (over y, core).
Axes of the slice: x: 4, y: 4, z: 8, core: 2. Of those that a mesh axis runs over, the one named last changes fastest.
Arguments:
- hidden_frames: bfloat16 [24576, 1280], P('dp', 'fsdp'), may hold values from -6 to 6
- conv_weight: bfloat16 [3, 1280, 1280], P(None, None, 'fsdp'), may hold values from -0.09375 to 0.09375
- conv_bias: bfloat16 [1280], P('fsdp'), may hold values from -4 to 4
- adapter_weight: bfloat16 [1280, 3584], P('fsdp'), may hold values from -0.15625 to 0.15625
- prompt_grad: bfloat16 [12288, 3584], P('dp'), may hold values from -6 to 6
- token_index: int32 [12288], P('dp'), may hold values from 0 to 12287, as said below
- clip_tokens: int32 [32, 6], P('dp'), may hold values from 1 to 256, 384 in all within a row
Outputs:
- grad_hidden: bfloat16 [24576, 1280], P('dp', 'fsdp')
- grad_adapter: float32 [1280, 3584], P('fsdp', 'dp')
- grad_conv: float32 [3, 1280, 1280], P(None, 'dp', 'fsdp')
The draws below stay inside these ranges and needn't reach their ends.
Inputs may be any that keep to these rules, and one draw needn't show every extreme that they name: `token_index`: each audio token appears exactly once. Token u belongs to index u // 384 of dp. The positions on one index of dp hold at most 24 tokens of any one index of dp, and some pair holds exactly 24. `clip_tokens`: each row sums to 384.
All inputs are finite; a program needn't handle non-finite values.
Results may differ from the reference program's by a relative error of at most 0.0049.
Values may be sent and summed in bfloat16 or wider, within the bound.
A program may use at most 128 MiB of HBM per device.

```python
import math
import jax
import jax.numpy as jnp
import numpy as np
from jax import lax

C = 1280
E = 3584
TOK_DEV = 384
CLIPS_DEV = 6
MOST_TOK = 256
GROUPS = 32
TOKENS = 12288
FRAMES = 24576
CAP = 24
N_DP = 32


def shuffle_rows(subkey):
    return jax.random.permutation(subkey, TOK_DEV)


def draw_token_index(key, part):
    key = jax.random.fold_in(key, 7)
    key_shift, key_delta, key_perm = jax.random.split(key, 3)
    shifts = jax.random.permutation(key_shift, N_DP)[:N_DP - 1].astype(jnp.int32)
    deltas = jax.random.randint(key_delta, (N_DP // 2 - 1,), 0, CAP // 4 + 1, dtype=jnp.int32)
    paired = jnp.stack([CAP // 2 + deltas, CAP // 2 - deltas], axis=1).reshape(-1)
    weights = jnp.concatenate([jnp.full((1,), CAP, jnp.int32), paired])
    block_ends = jnp.cumsum(weights).astype(jnp.int32)
    row_tokens = jax.vmap(shuffle_rows)(jax.random.split(key_perm, N_DP)).astype(jnp.int32)
    blocks = jnp.sum((row_tokens[:, :, None] >= block_ends[None, None, :]).astype(jnp.int32), axis=2)
    senders = jnp.arange(N_DP, dtype=jnp.int32)[:, None]
    owners = jnp.mod(senders - shifts[blocks], N_DP)
    return (owners * TOK_DEV + row_tokens).reshape(-1).astype(jnp.int32)


def with_spikes(array, rng, source, target, blocks, factor):
    owner, partner = [(jnp.arange(array.shape[dim]) // (array.shape[dim] // blocks)).reshape([-1 if axis == dim else 1 for axis in range(array.ndim)]) for dim in (source, target)]
    chosen = jax.random.permutation(rng, blocks)[partner]
    strong = (owner == chosen) | (owner == (partner + blocks // 2) % blocks)
    return jnp.where(strong, factor * array, array)


def block_scale(key, dims, shards, low, high):
    loudness = 1.0
    for dim, parts in shards:
        steps = jax.random.uniform(jax.random.fold_in(jax.random.fold_in(key, 6), dim), (parts,), jnp.float32, low / len(shards), high / len(shards))
        loudness = loudness * jnp.repeat(jnp.exp(steps), dims[dim] // parts).reshape((-1,) + (1,) * (len(dims) - 1 - dim))
    return loudness


def split_up(number_of, total, most, skew):
    loads = [(1 << 20) // math.isqrt(rank ** skew) + 1 for rank in range(2, number_of + 1)]
    spare, counts = total - most - (number_of - 1), [1] * (number_of - 1)
    while spare > 0:
        free = [i for i in range(number_of - 1) if counts[i] < most]
        whole, budget = sum([loads[i] for i in free]), spare
        for i in free:
            extra = min(most - counts[i], max(1, budget * loads[i] // whole), spare)
            counts[i] = counts[i] + extra
            spare = spare - extra
    return np.array([most] + counts)


def uneven_parts(own_key, amount, total, limit, skew):
    if amount == 2:
        one = jax.random.randint(own_key, (), max(1, total - limit), min(limit, total - 1) + 1)
        return jnp.stack([one, total - one])
    lengths = jnp.asarray(split_up(amount, total, limit, skew), jnp.int32)
    couples = (amount - 1) // 2
    donor, receiver = lengths[1:1 + 2 * couples:2], lengths[2:2 + 2 * couples:2]
    slack = jnp.minimum(donor - 1, limit - receiver)
    passed = jax.random.randint(jax.random.fold_in(own_key, 1), (couples,), 0, 1 << 20) % (slack + 1)
    lengths = lengths.at[1:1 + 2 * couples:2].set(donor - passed).at[2:2 + 2 * couples:2].set(receiver + passed)
    return lengths[jax.random.permutation(jax.random.fold_in(own_key, 2), amount)]


def centred(key, dims, deviation, reach, cuts=(), kind=jnp.bfloat16):
    level = block_scale(key, dims, cuts, -0.22, 0.18) if cuts else 1.0
    array = jax.random.normal(key, dims, jnp.float32) * deviation * level
    return jnp.minimum(jnp.maximum(array, -reach), reach).astype(kind)


def noise_with(own_key, extent, spread, reach, cuts, heavy, held_as=jnp.bfloat16):
    values = spread * jax.random.normal(own_key, extent, jnp.float32)
    if cuts:
        values = values * block_scale(own_key, extent, cuts, -0.22, 0.18)
    return jnp.clip(with_spikes(values, jax.random.fold_in(own_key, 3), *heavy), -reach, reach).astype(held_as)


def setup_inputs(seed: int = 0) -> dict:
    key_list = jax.random.split(jax.random.key(seed), 8)
    return {
        "hidden_frames": centred(key_list[0], (FRAMES, C), 1.0, 6.0, ((0, 32), (1, 8))),
        "conv_weight": centred(key_list[1], (3, C, C), (3 * C) ** -0.5, 0.09375, ((2, 8),)),
        "conv_bias": centred(key_list[2], (C,), 0.7, 4.0, ((0, 8),)),
        "adapter_weight": centred(key_list[3], (C, E), C ** -0.5, 0.15625, ((0, 8),)),
        "prompt_grad": noise_with(key_list[4], (TOKENS, E), 1.0, 6.0, ((0, 32),), (0, 1, 32, 2.75)),
        "token_index": draw_token_index(jax.random.fold_in(key_list[7], 71), 0),
        "clip_tokens": jax.vmap(lambda own: uneven_parts(own, CLIPS_DEV, TOK_DEV, MOST_TOK, 2))(jax.random.split(key_list[6], GROUPS)).reshape((GROUPS, CLIPS_DEV)).astype(jnp.int32),
    }


def gelu_slope(preact):
    return 0.5 * (1.0 + jax.scipy.special.erf(preact / math.sqrt(2.0))) + preact * jnp.exp(-0.5 * preact * preact) / math.sqrt(2.0 * math.pi)

def contract_last(left_rows, right_rows):
    return lax.dot_general(left_rows, right_rows, (((1,), (1,)), ((), ())), preferred_element_type=jnp.float32)

def frame_grads(slope_rows, weights, inside):
    even_part = contract_last(slope_rows, weights[1])
    odd_part = contract_last(slope_rows, weights[2])
    early_part = contract_last(slope_rows, weights[0]) * inside[:, None]
    shifted = jnp.concatenate([early_part[1:], jnp.zeros((1, early_part.shape[1]), jnp.float32)], axis=0)
    odd_part = odd_part + shifted
    return jnp.stack([even_part, odd_part], axis=1).reshape(2 * slope_rows.shape[0], even_part.shape[1])

def forward_parts(frames, inside, conv_weight, conv_bias):
    paired = frames.reshape(frames.shape[0] // 2, 2, frames.shape[1])
    even_frames = paired[:, 0]
    odd_frames = paired[:, 1]
    earlier = jnp.concatenate([jnp.zeros((1, frames.shape[1]), jnp.bfloat16), odd_frames[:-1]], axis=0)
    earlier = earlier * inside.astype(jnp.bfloat16)[:, None]
    preact = jnp.dot(earlier, conv_weight[0], preferred_element_type=jnp.float32)
    preact = preact + jnp.dot(even_frames, conv_weight[1], preferred_element_type=jnp.float32)
    preact = preact + jnp.dot(odd_frames, conv_weight[2], preferred_element_type=jnp.float32)
    preact = preact + conv_bias.astype(jnp.float32)[None, :]
    return (earlier, even_frames, odd_frames, preact)

def reference(hidden_frames, conv_weight, conv_bias, adapter_weight, prompt_grad, token_index, clip_tokens):
    token_grad = jnp.zeros((TOKENS, E), jnp.bfloat16).at[token_index].set(prompt_grad)
    offsets = (jnp.arange(N_DP, dtype=jnp.int32) * TOK_DEV)[:, None]
    starts = (jnp.cumsum(clip_tokens, axis=1) - clip_tokens).astype(jnp.int32) + offsets
    inside = jnp.ones((TOKENS,), jnp.float32).at[starts.reshape(-1)].set(0.0)
    earlier, even_frames, odd_frames, preact = forward_parts(hidden_frames, inside, conv_weight, conv_bias)
    hidden_out = jax.nn.gelu(preact, approximate=False).astype(jnp.bfloat16)
    back_hidden = contract_last(token_grad, adapter_weight)
    slope_rows = (back_hidden * gelu_slope(preact)).astype(jnp.bfloat16)
    grad_scale = 1.0 / math.sqrt(TOKENS)
    grad_adapter = jnp.dot(hidden_out.T, token_grad, preferred_element_type=jnp.float32) * grad_scale
    grad_conv = jnp.stack([jnp.dot(source.T, slope_rows, preferred_element_type=jnp.float32) for source in (earlier, even_frames, odd_frames)]) * grad_scale
    grad_hidden = frame_grads(slope_rows, conv_weight, inside).astype(jnp.bfloat16)
    return (grad_hidden, grad_adapter, grad_conv)
```

```python
import math

import jax
import jax.numpy as jnp
from jax import lax
from jax.experimental import pallas as pl
from jax.experimental.pallas import tpu as pltpu
from jax.sharding import PartitionSpec as P

MESH = pl.DeviceIdType.MESH
F32 = jnp.float32
BF16 = jnp.bfloat16

NX, NZ, NY = 4, 8, 4
N_DP, N_FSDP = NX * NZ, 2 * NY
TOK = 384
CH = 160
WIDTH = 3584
CAP = 24
LOW = 128
ECOL, EPAD = WIDTH // N_DP, 128
TAPC = 40
GRAD_SCALE = 1.0 / math.sqrt(TOK * N_DP)


def nn(left, right):
    return lax.dot_general(left, right, (((1,), (0,)), ((), ())), preferred_element_type=F32)


def nt(left, right):
    return lax.dot_general(left, right, (((1,), (1,)), ((), ())), preferred_element_type=F32)


def iota(shape, dim):
    return lax.broadcasted_iota(jnp.int32, shape, dim)


def pick(cond):
    return jnp.where(cond, 1.0, 0.0).astype(F32)


def low_hot(keys):
    rows = iota((N_DP, CAP, TOK), 1)
    return pick(keys[:, None, :] == rows).reshape(N_DP * CAP, TOK).astype(BF16)


def high_hot(keys, group):
    rows = iota((N_DP, 8, TOK), 1)
    hit = (keys[:, None, :] == rows + 6 * group) & (rows < 6)
    return pick(hit).reshape(N_DP * 8, TOK).astype(BF16)


def pack(low_ref, high_ref, rows_t, extra=None):
    low = nt(low_ref[...], rows_t[:LOW])
    tail = rows_t[LOW:]
    zero = jnp.zeros((CH - LOW, TOK), BF16)
    high = extra
    for group in range(4):
        placed = jnp.concatenate([tail if g == group else zero for g in range(4)], axis=0)
        part = nt(high_ref[group], placed)
        high = part if high is None else high + part
    slabs = jnp.concatenate([low.reshape(N_DP, CAP, 128), high.reshape(N_DP, 8, 128)], axis=1)
    return slabs.astype(BF16)


def unpack(low_ref, high_ref, got):
    got = got.astype(F32)
    low = got[:, :CAP, :].reshape(N_DP * CAP, 128).T.astype(BF16)
    high = got[:, CAP:, :].reshape(N_DP * 8, 128).T.astype(BF16)
    low = nn(low, low_ref[...])
    tail = None
    for group in range(4):
        part = nn(high[32 * group : 32 * group + 32], high_ref[group])
        tail = part if tail is None else tail + part
    return jnp.concatenate([low, tail], axis=0)


def kernel(
    frames_ref, weight_ref, bias_ref, adapter_ref, prompt_ref, index_ref, clips_ref,
    hidden_ref, gadapter_ref, gconv_ref,
    prompt_pad, weight_t, weight_in, weight_own, xown, xbuf,
    slow, shigh, dlow, dhigh, send, got, slope_all,
    parts, rs_in, rs_out, zsend, zgot, totals,
    route_ss, route_rs, ag_ss, ag_rs, w_ss, w_rs, rs_ss, rs_rs, z_ss, z_rs,
):
    d = lax.axis_index("dp")
    f = lax.axis_index("fsdp")
    x, z = d // NZ, lax.rem(d, NZ)
    y, c = f // 2, lax.rem(f, 2)
    pending = []

    def at(dp, fs):
        return {"dp": dp, "fsdp": fs}

    def rcopy(src, dst, ssem, rsem, dev):
        return pltpu.make_async_remote_copy(
            src_ref=src, dst_ref=dst, send_sem=ssem, recv_sem=rsem,
            device_id=dev, device_id_type=MESH,
        )

    def go(src, dst, ssem, rsem, dev):
        copy = rcopy(src, dst, ssem, rsem, dev)
        copy.start()
        pending.append(copy)

    def arrived(dst, ssem, rsem):
        rcopy(dst, dst, ssem, rsem, at(d, f)).wait_recv()

    barrier = pltpu.get_barrier_semaphore()

    def greet_dp(k, carry):
        pl.semaphore_signal(
            barrier, inc=1, device_id=at(lax.rem(d + k, N_DP), f), device_id_type=MESH
        )
        return carry

    def greet_fsdp(k, carry):
        pl.semaphore_signal(
            barrier, inc=1, device_id=at(d, lax.rem(f + k, N_FSDP)), device_id_type=MESH
        )
        return carry

    lax.fori_loop(1, N_DP, greet_dp, 0)
    lax.fori_loop(1, N_FSDP, greet_fsdp, 0)

    row = iota((2 * TOK, 2 * TOK), 0)
    col = iota((2 * TOK, 2 * TOK), 1)
    source = jnp.where(row < TOK, 2 * row + 1, 2 * (row - TOK))
    frames_t = nn(pick(col == source).astype(BF16), frames_ref[...]).T
    for q in range(4):
        lines = frames_t[TAPC * q : TAPC * q + TAPC]
        xown[q] = jnp.concatenate([lines[:, :TOK], lines[:, TOK:]], axis=0).astype(BF16)

    pl.semaphore_wait(barrier, N_DP - 1 + N_FSDP - 1)

    yr, yl, yo = lax.rem(y + 1, NY), lax.rem(y + NY - 1, NY), lax.rem(y + 2, NY)

    class Gather:
        def __init__(self, which, own, block, half):
            self.ss, self.rs = ag_ss.at[which], ag_rs.at[which]
            self.own, self.block, self.half = own, block, half

        def send(self, src, dst, k, dev):
            go(src, dst, self.ss.at[k], self.rs.at[k], dev)

        def first(self):
            here = self.block(f)
            self.send(self.own, here, 0, at(d, yr * 2 + c))
            self.send(self.own, here, 1, at(d, yl * 2 + c))
            self.send(self.own, here, 2, at(d, y * 2 + 1 - c))

        def relay(self):
            mate = at(d, y * 2 + 1 - c)
            left, right = yl * 2 + c, yr * 2 + c
            arrived(self.block(left), self.ss.at[0], self.rs.at[0])
            self.send(self.half(left, 0), self.half(left, 0), 3, at(d, yr * 2 + c))
            self.send(self.block(left), self.block(left), 5, mate)
            arrived(self.block(right), self.ss.at[1], self.rs.at[1])
            self.send(self.half(right, 1), self.half(right, 1), 4, at(d, yl * 2 + c))
            self.send(self.block(right), self.block(right), 6, mate)

        def share(self):
            mate = at(d, y * 2 + 1 - c)
            far = yo * 2 + c
            arrived(self.half(far, 0), self.ss.at[3], self.rs.at[3])
            self.send(self.half(far, 0), self.half(far, 0), 7, mate)
            arrived(self.half(far, 1), self.ss.at[4], self.rs.at[4])
            self.send(self.half(far, 1), self.half(far, 1), 8, mate)

        def last(self):
            o = 1 - c
            arrived(self.block(y * 2 + o), self.ss.at[2], self.rs.at[2])
            arrived(self.block(yl * 2 + o), self.ss.at[5], self.rs.at[5])
            arrived(self.block(yr * 2 + o), self.ss.at[6], self.rs.at[6])
            arrived(self.half(yo * 2 + o, 0), self.ss.at[7], self.rs.at[7])
            arrived(self.half(yo * 2 + o, 1), self.ss.at[8], self.rs.at[8])

    frames_ag = Gather(
        0,
        xown,
        lambda g: xbuf.at[pl.ds(4 * g, 4), pl.ds(0, 80), :],
        lambda g, h: xbuf.at[pl.ds(4 * g + 2 * h, 2), pl.ds(0, 80), :],
    )
    frames_ag.first()
    xbuf[pl.ds(4 * f, 4), pl.ds(0, 80), :] = xown[...]

    index = index_ref[...]
    group = iota((N_DP, TOK), 0)
    mine = (index >= group * TOK) & (index < (group + 1) * TOK)
    member = pick(mine)
    before = pick(iota((TOK, TOK), 0) < iota((TOK, TOK), 1)).astype(BF16)
    rank = nn(member.astype(BF16), before)
    local = index - jnp.sum(jnp.where(mine, group, 0), axis=0, keepdims=True) * TOK
    keys = jnp.where(mine, rank.astype(jnp.int32), -1)
    slow[...] = low_hot(keys)
    for g in range(4):
        shigh[g] = high_hot(keys, g)
    own_rank = jnp.max(keys, axis=0, keepdims=True)
    by_rank = pick(iota((128, TOK), 0) == own_rank).astype(BF16)
    part = iota((N_DP, 8, TOK), 1)
    high_bits = jnp.where(mine, (local >> 4) + 1, 0).astype(F32)
    low_bits = jnp.where(mine, local & 15, 0).astype(F32)
    marks = jnp.where(part == 6, high_bits[:, None, :], jnp.where(part == 7, low_bits[:, None, :], 0.0))
    extra = nt(marks.reshape(N_DP * 8, TOK).astype(BF16), by_rank)

    back_t = nt(adapter_ref[...], prompt_ref[...]).astype(BF16)
    send[0] = pack(slow, shigh, back_t, extra)

    def route(which):
        def step(k, carry):
            to = lax.rem(d + k, N_DP)
            rcopy(
                send.at[which, to], got.at[which, d],
                route_ss.at[which, k], route_rs.at[which, k], at(to, f),
            ).start()
            return carry

        lax.fori_loop(1, N_DP, step, 0)
        got[which, pl.ds(d, 1)] = send[which, pl.ds(d, 1)]

    def routed(which):
        def step(k, carry):
            come = lax.rem(d + N_DP - k, N_DP)
            rcopy(
                got.at[which, come], got.at[which, come],
                route_ss.at[which, k], route_rs.at[which, k], at(come, f),
            ).wait_recv()
            return carry

        lax.fori_loop(1, N_DP, step, 0)

    def route_sent(which):
        def step(k, carry):
            to = lax.rem(d + k, N_DP)
            rcopy(
                send.at[which, to], got.at[which, d],
                route_ss.at[which, k], route_rs.at[which, k], at(to, f),
            ).wait_send()
            return carry

        lax.fori_loop(1, N_DP, step, 0)

    route(0)
    frames_ag.relay()

    pad8 = jnp.zeros((8, CH), F32)
    for o in range(N_DP):
        lines = [weight_ref[k, TAPC * o : TAPC * o + TAPC, :].astype(F32) for k in (2, 1, 0)]
        weight_t[:, 128 * o : 128 * o + 128] = jnp.concatenate(lines + [pad8], axis=0).T.astype(BF16)

    frames_ag.share()

    for o in range(N_DP):
        columns = prompt_ref[:, ECOL * o : ECOL * o + ECOL]
        prompt_pad[:, 128 * o : 128 * o + 128] = jnp.concatenate(
            [columns, jnp.zeros((TOK, 128 - ECOL), BF16)], axis=1
        )

    lane = iota((1, TOK), 1)
    inside = jnp.ones((1, TOK), F32)
    start = jnp.int32(0)
    for k in range(6):
        inside = jnp.where(lane == start, 0.0, inside)
        start = start + clips_ref[0, k]

    frames_ag.last()

    def weight_out(k, carry):
        to = lax.rem(f + k, N_FSDP)
        rcopy(
            weight_t.at[:, pl.ds(pl.multiple_of(to * 512, 512), 512)], weight_in.at[f],
            w_ss.at[k], w_rs.at[k], at(d, to),
        ).start()
        return carry

    lax.fori_loop(1, N_FSDP, weight_out, 0)
    weight_in[pl.ds(f, 1)] = weight_t[:, pl.ds(pl.multiple_of(f * 512, 512), 512)][None]

    live = pick(iota((48, TOK), 0) < TAPC) * inside

    def shift_in(o, carry):
        lines = xbuf[pl.ds(o, 1), pl.ds(0, 48), :][0].astype(F32)
        xbuf[pl.ds(o, 1), pl.ds(80, 48), :] = (pltpu.roll(lines, 1, 1) * live).astype(BF16)[None]
        return carry

    lax.fori_loop(0, N_DP, shift_in, 0)

    preact = nn(weight_t[...], xbuf[...].reshape(N_DP * 128, TOK)) + bias_ref[...].astype(F32)
    cumul = 0.5 * (1.0 + lax.erf(preact * (1.0 / math.sqrt(2.0))))
    hidden_t = (preact * cumul).astype(BF16)
    slope = cumul + preact * jnp.exp(-0.5 * preact * preact) * (1.0 / math.sqrt(2.0 * math.pi))

    routed(0)
    tags = got[0, :, CAP:, :].astype(F32)
    numbers = (tags[:, 6, :] - 1.0) * 16.0 + tags[:, 7, :]

    def token_of(rows, first, most):
        spot = iota((N_DP, rows, 128), 1)
        match = (iota((N_DP, rows, 128), 2) == spot + first) & (spot < most)
        picked = jnp.sum(jnp.where(match, numbers[:, None, :], 0.0), axis=2, keepdims=True)
        ok = iota((N_DP, rows, 1), 1) < most
        return jnp.where(ok, picked, -1.0)

    def token_hot(rows, first, most):
        token = iota((N_DP, rows, TOK), 2).astype(F32)
        return pick(token_of(rows, first, most) == token).reshape(N_DP * rows, TOK).astype(BF16)

    dlow[...] = token_hot(CAP, 0, CAP)
    for g in range(4):
        dhigh[g] = token_hot(8, 6 * g, 6)
    send[1] = pack(dlow, dhigh, hidden_t)
    route(1)

    slope_t = (unpack(dlow, dhigh, got[0]) * slope).astype(BF16)
    slope_all[pl.ds(f, 1)] = slope_t[None]
    slope_ag = Gather(
        1,
        slope_all.at[f],
        lambda g: slope_all.at[g],
        lambda g, h: slope_all.at[g, pl.ds(80 * h, 80), :],
    )
    slope_ag.first()

    xr, xl, xo = lax.rem(x + 1, NX), lax.rem(x + NX - 1, NX), lax.rem(x + 2, NX)
    to_right, to_left = at(xr * NZ + z, f), at(xl * NZ + z, f)

    def halves(which, owner, h):
        return parts.at[which, pl.ds(owner * NZ + 4 * h, 4)]

    def rs_send(which, src, k, dev):
        go(src, rs_in.at[which, k], rs_ss.at[which, k], rs_rs.at[which, k], dev)

    def rs_wait(which, k):
        arrived(rs_in.at[which, k], rs_ss.at[which, k], rs_rs.at[which, k])

    def rs_first(which):
        rs_send(which, halves(which, xo, 0), 0, to_right)
        rs_send(which, halves(which, xo, 1), 1, to_left)
        rs_send(which, halves(which, xr, 1), 2, to_right)
        rs_send(which, halves(which, xl, 0), 3, to_left)

    def rs_second(which):
        rs_wait(which, 0)
        rs_out[which, 0] = (halves(which, xr, 0)[...].astype(F32) + rs_in[which, 0].astype(F32)).astype(BF16)
        rs_send(which, rs_out.at[which, 0], 4, to_right)
        rs_wait(which, 1)
        rs_out[which, 1] = (halves(which, xl, 1)[...].astype(F32) + rs_in[which, 1].astype(F32)).astype(BF16)
        rs_send(which, rs_out.at[which, 1], 5, to_left)

    def rs_third(which):
        for k in (2, 3, 4, 5):
            rs_wait(which, k)
        for h, (one, two) in enumerate(((4, 3), (5, 2))):
            total = halves(which, x, h)[...].astype(F32) + rs_in[which, one].astype(F32)
            total = total + rs_in[which, two].astype(F32)
            totals[which, pl.ds(4 * h, 4)] = total
            zsend[which, pl.ds(4 * h, 4)] = total.astype(BF16)

        def step(k, carry):
            to = lax.rem(z + k, NZ)
            rcopy(
                zsend.at[which, to], zgot.at[which, k],
                z_ss.at[which, k], z_rs.at[which, k], at(x * NZ + to, f),
            ).start()
            return carry

        lax.fori_loop(1, NZ, step, 0)

    def rs_last(which):
        total = totals[which, pl.ds(z, 1)][0]
        for k in range(1, NZ):
            arrived(zgot.at[which, k], z_ss.at[which, k], z_rs.at[which, k])
            total = total + zgot[which, k].astype(F32)
        return total * GRAD_SCALE

    def conv_part(o, carry):
        block = xbuf[pl.ds(o, 1)][0]
        parts[0, pl.ds(o, 1)] = nt(slope_all[pl.ds(f, 1)][0], block).astype(BF16)[None]
        return carry

    lax.fori_loop(0, N_DP, conv_part, 0)
    rs_first(0)
    slope_ag.relay()

    routed(1)
    hidden_pos = unpack(slow, shigh, got[1]).astype(BF16)
    for o in range(N_DP):
        parts[1, o] = nn(hidden_pos, prompt_pad[:, 128 * o : 128 * o + 128]).astype(BF16)
    rs_first(1)
    slope_ag.share()
    rs_second(0)

    def weight_come(k, carry):
        come = lax.rem(f + N_FSDP - k, N_FSDP)
        rcopy(
            weight_in.at[come], weight_in.at[come], w_ss.at[k], w_rs.at[k], at(d, come)
        ).wait_recv()
        return carry

    lax.fori_loop(1, N_FSDP, weight_come, 0)
    for g in range(N_FSDP):
        weight_own[:, CH * g : CH * g + CH] = weight_in[g].T
    rs_second(1)
    slope_ag.last()
    grads = nn(weight_own[...], slope_all[...].reshape(N_FSDP * CH, TOK))
    odd, even = [], []
    for q in range(4):
        lines = grads[128 * q : 128 * q + 128]
        odd.append(lines[:TAPC] + pltpu.roll(lines[2 * TAPC : 3 * TAPC] * inside, TOK - 1, 1))
        even.append(lines[TAPC : 2 * TAPC])
    both = jnp.concatenate([jnp.concatenate(odd, axis=0), jnp.concatenate(even, axis=0)], axis=1)
    row = iota((2 * TOK, 2 * TOK), 0)
    col = iota((2 * TOK, 2 * TOK), 1)
    place = jnp.where(col < TOK, 2 * col + 1, 2 * (col - TOK))
    hidden_ref[...] = nt(pick(row == place).astype(BF16), both.astype(BF16)).astype(BF16)

    rs_third(0)
    rs_third(1)
    conv = rs_last(0).T
    gconv_ref[0] = conv[2 * TAPC : 3 * TAPC]
    gconv_ref[1] = conv[TAPC : 2 * TAPC]
    gconv_ref[2] = conv[:TAPC]
    gadapter_ref[...] = rs_last(1)[:, :ECOL]

    for copy in pending:
        copy.wait_send()
    route_sent(0)
    route_sent(1)

    def weight_sent(k, carry):
        to = lax.rem(f + k, N_FSDP)
        rcopy(
            weight_t.at[:, pl.ds(pl.multiple_of(to * 512, 512), 512)], weight_in.at[f],
            w_ss.at[k], w_rs.at[k], at(d, to),
        ).wait_send()
        return carry

    lax.fori_loop(1, N_FSDP, weight_sent, 0)

    def z_sent(k, carry):
        to = lax.rem(z + k, NZ)
        for which in range(2):
            rcopy(
                zsend.at[which, to], zgot.at[which, k],
                z_ss.at[which, k], z_rs.at[which, k], at(x * NZ + to, f),
            ).wait_send()
        return carry

    lax.fori_loop(1, NZ, z_sent, 0)


def body(
    hidden_frames, conv_weight, conv_bias, adapter_weight, prompt_grad, token_index, clip_tokens
):
    vmem = pl.BlockSpec(memory_space=pltpu.VMEM)
    dma = pltpu.SemaphoreType.DMA
    return pl.pallas_call(
        kernel,
        out_shape=(
            jax.ShapeDtypeStruct((2 * TOK, CH), BF16),
            jax.ShapeDtypeStruct((CH, ECOL), F32),
            jax.ShapeDtypeStruct((3, TAPC, CH), F32),
        ),
        in_specs=[vmem] * 6 + [pl.BlockSpec(memory_space=pltpu.SMEM)],
        out_specs=(vmem, vmem, vmem),
        scratch_shapes=[
            pltpu.VMEM((TOK, N_DP * EPAD), BF16),
            pltpu.VMEM((CH, N_DP * 128), BF16),
            pltpu.VMEM((N_FSDP, CH, 512), BF16),
            pltpu.VMEM((512, N_FSDP * CH), BF16),
            pltpu.VMEM((4, 80, TOK), BF16),
            pltpu.VMEM((N_DP, 128, TOK), BF16),
            pltpu.VMEM((N_DP * CAP, TOK), BF16),
            pltpu.VMEM((4, N_DP * 8, TOK), BF16),
            pltpu.VMEM((N_DP * CAP, TOK), BF16),
            pltpu.VMEM((4, N_DP * 8, TOK), BF16),
            pltpu.VMEM((2, N_DP, 32, 128), BF16),
            pltpu.VMEM((2, N_DP, 32, 128), BF16),
            pltpu.VMEM((N_FSDP, CH, TOK), BF16),
            pltpu.VMEM((2, N_DP, CH, 128), BF16),
            pltpu.VMEM((2, 6, 4, CH, 128), BF16),
            pltpu.VMEM((2, 2, 4, CH, 128), BF16),
            pltpu.VMEM((2, NZ, CH, 128), BF16),
            pltpu.VMEM((2, NZ, CH, 128), BF16),
            pltpu.VMEM((2, NZ, CH, 128), F32),
            dma((2, N_DP)), dma((2, N_DP)),
            dma((2, 9)), dma((2, 9)),
            dma((N_FSDP,)), dma((N_FSDP,)),
            dma((2, 6)), dma((2, 6)),
            dma((2, NZ)), dma((2, NZ)),
        ],
        compiler_params=pltpu.CompilerParams(
            collective_id=0, has_side_effects=True, vmem_limit_bytes=56 * 1024 * 1024
        ),
    )(
        hidden_frames,
        conv_weight,
        conv_bias.reshape(CH, 1),
        adapter_weight,
        prompt_grad,
        token_index.reshape(1, TOK),
        clip_tokens,
    )


def solution(mesh):
    placed = (
        P("dp", "fsdp"),
        P(None, None, "fsdp"),
        P("fsdp"),
        P("fsdp", None),
        P("dp", None),
        P("dp"),
        P("dp", None),
    )
    return jax.shard_map(
        body,
        mesh=mesh,
        in_specs=placed,
        out_specs=(P("dp", "fsdp"), P("fsdp", "dp"), P(None, "dp", "fsdp")),
        check_vma=False,
    )
```

```python
import math

import jax
import jax.numpy as jnp
from jax import lax
from jax.experimental import pallas as pl
from jax.experimental.pallas import tpu as pltpu
from jax.sharding import PartitionSpec as P

MESH = pl.DeviceIdType.MESH
F32 = jnp.float32
BF16 = jnp.bfloat16

NX, NZ, NY = 4, 8, 4
N_DP, N_FSDP = NX * NZ, 2 * NY
TOK = 384
CH = 160
WIDTH = 3584
CAP = 24
LOW = 128
ECOL, EPAD = WIDTH // N_DP, 128
TAPC = 40
GRAD_SCALE = 1.0 / math.sqrt(TOK * N_DP)


def nn(left, right):
    return lax.dot_general(left, right, (((1,), (0,)), ((), ())), preferred_element_type=F32)


def nt(left, right):
    return lax.dot_general(left, right, (((1,), (1,)), ((), ())), preferred_element_type=F32)


def iota(shape, dim):
    return lax.broadcasted_iota(jnp.int32, shape, dim)


def pick(cond):
    return jnp.where(cond, 1.0, 0.0).astype(F32)


def low_hot(keys):
    rows = iota((N_DP, CAP, TOK), 1)
    return pick(keys[:, None, :] == rows).reshape(N_DP * CAP, TOK).astype(BF16)


def high_hot(keys, group):
    rows = iota((N_DP, 8, TOK), 1)
    hit = (keys[:, None, :] == rows + 6 * group) & (rows < 6)
    return pick(hit).reshape(N_DP * 8, TOK).astype(BF16)


def pack(low_ref, high_ref, rows_t, extra=None):
    low = nt(low_ref[...], rows_t[:LOW])
    tail = rows_t[LOW:]
    zero = jnp.zeros((CH - LOW, TOK), BF16)
    high = extra
    for group in range(4):
        placed = jnp.concatenate([tail if g == group else zero for g in range(4)], axis=0)
        part = nt(high_ref[group], placed)
        high = part if high is None else high + part
    slabs = jnp.concatenate([low.reshape(N_DP, CAP, 128), high.reshape(N_DP, 8, 128)], axis=1)
    return slabs.astype(BF16)


def unpack(low_ref, high_ref, got):
    got = got.astype(F32)
    low = got[:, :CAP, :].reshape(N_DP * CAP, 128).T.astype(BF16)
    high = got[:, CAP:, :].reshape(N_DP * 8, 128).T.astype(BF16)
    low = nn(low, low_ref[...])
    tail = None
    for group in range(4):
        part = nn(high[32 * group : 32 * group + 32], high_ref[group])
        tail = part if tail is None else tail + part
    return jnp.concatenate([low, tail], axis=0)


def kernel(
    frames_hbm, weight_hbm, bias_ref, adapter_hbm, prompt_hbm, index_ref, clips_ref,
    hidden_ref, sums_ref,
    frames_ref, weight_ref, adapter_ref, prompt_ref, in_sem, halving,
    prompt_pad, weight_t, weight_in, weight_own, xown, xbuf,
    slow, shigh, dlow, dhigh, send, got, slope_all,
    parts, rs_in, rs_out, zsend, zgot, totals,
    route_ss, route_rs, ag_ss, ag_rs, w_ss, w_rs, rs_ss, rs_rs, z_ss, z_rs,
):
    d = lax.axis_index("dp")
    f = lax.axis_index("fsdp")
    x, z = d // NZ, lax.rem(d, NZ)
    y, c = f // 2, lax.rem(f, 2)
    pending = []
    loads = [
        pltpu.make_async_copy(src, dst, in_sem.at[k])
        for k, (src, dst) in enumerate(
            (
                (frames_hbm, frames_ref),
                (adapter_hbm, adapter_ref),
                (prompt_hbm, prompt_ref),
                (weight_hbm, weight_ref),
            )
        )
    ]
    for load in loads:
        load.start()

    def at(dp, fs):
        return {"dp": dp, "fsdp": fs}

    def rcopy(src, dst, ssem, rsem, dev):
        return pltpu.make_async_remote_copy(
            src_ref=src, dst_ref=dst, send_sem=ssem, recv_sem=rsem,
            device_id=dev, device_id_type=MESH,
        )

    def go(src, dst, ssem, rsem, dev):
        copy = rcopy(src, dst, ssem, rsem, dev)
        copy.start()
        pending.append(copy)

    def arrived(dst, ssem, rsem):
        rcopy(dst, dst, ssem, rsem, at(d, f)).wait_recv()

    barrier = pltpu.get_barrier_semaphore()

    def greet_dp(k, carry):
        pl.semaphore_signal(
            barrier, inc=1, device_id=at(lax.rem(d + k, N_DP), f), device_id_type=MESH
        )
        return carry

    def greet_fsdp(k, carry):
        pl.semaphore_signal(
            barrier, inc=1, device_id=at(d, lax.rem(f + k, N_FSDP)), device_id_type=MESH
        )
        return carry

    lax.fori_loop(1, N_DP, greet_dp, 0)
    lax.fori_loop(1, N_FSDP, greet_fsdp, 0)

    row = iota((256, 256), 0)
    col = iota((256, 256), 1)
    halving[...] = pick(row == jnp.where(col < 128, 2 * col + 1, 2 * (col - 128))).astype(BF16)
    loads[0].wait()
    for b in range(3):
        lines = nn(frames_ref[:, 256 * b : 256 * b + 256], halving[...])
        for q in range(4):
            quarter = lines[TAPC * q : TAPC * q + TAPC]
            xown[q, :, 128 * b : 128 * b + 128] = jnp.concatenate(
                [quarter[:, :128], quarter[:, 128:]], axis=0
            ).astype(BF16)

    pl.semaphore_wait(barrier, N_DP - 1 + N_FSDP - 1)

    yr, yl, yo = lax.rem(y + 1, NY), lax.rem(y + NY - 1, NY), lax.rem(y + 2, NY)

    class Gather:
        def __init__(self, which, own, block, half):
            self.ss, self.rs = ag_ss.at[which], ag_rs.at[which]
            self.own, self.block, self.half = own, block, half

        def send(self, src, dst, k, dev):
            go(src, dst, self.ss.at[k], self.rs.at[k], dev)

        def first(self):
            here = self.block(f)
            self.send(self.own, here, 0, at(d, yr * 2 + c))
            self.send(self.own, here, 1, at(d, yl * 2 + c))
            self.send(self.own, here, 2, at(d, y * 2 + 1 - c))

        def relay(self):
            mate = at(d, y * 2 + 1 - c)
            left, right = yl * 2 + c, yr * 2 + c
            arrived(self.block(left), self.ss.at[0], self.rs.at[0])
            self.send(self.half(left, 0), self.half(left, 0), 3, at(d, yr * 2 + c))
            self.send(self.block(left), self.block(left), 5, mate)
            arrived(self.block(right), self.ss.at[1], self.rs.at[1])
            self.send(self.half(right, 1), self.half(right, 1), 4, at(d, yl * 2 + c))
            self.send(self.block(right), self.block(right), 6, mate)

        def share(self):
            mate = at(d, y * 2 + 1 - c)
            far = yo * 2 + c
            arrived(self.half(far, 0), self.ss.at[3], self.rs.at[3])
            self.send(self.half(far, 0), self.half(far, 0), 7, mate)
            arrived(self.half(far, 1), self.ss.at[4], self.rs.at[4])
            self.send(self.half(far, 1), self.half(far, 1), 8, mate)

        def last(self):
            o = 1 - c
            arrived(self.block(y * 2 + o), self.ss.at[2], self.rs.at[2])
            arrived(self.block(yl * 2 + o), self.ss.at[5], self.rs.at[5])
            arrived(self.block(yr * 2 + o), self.ss.at[6], self.rs.at[6])
            arrived(self.half(yo * 2 + o, 0), self.ss.at[7], self.rs.at[7])
            arrived(self.half(yo * 2 + o, 1), self.ss.at[8], self.rs.at[8])

    frames_ag = Gather(
        0,
        xown,
        lambda g: xbuf.at[pl.ds(4 * g, 4), pl.ds(0, 80), :],
        lambda g, h: xbuf.at[pl.ds(4 * g + 2 * h, 2), pl.ds(0, 80), :],
    )
    frames_ag.first()
    xbuf[pl.ds(4 * f, 4), pl.ds(0, 80), :] = xown[...]

    index = index_ref[...].reshape(1, TOK)
    group = iota((N_DP, TOK), 0)
    mine = (index >= group * TOK) & (index < (group + 1) * TOK)
    member = pick(mine)
    before = pick(iota((TOK, TOK), 0) < iota((TOK, TOK), 1)).astype(BF16)
    rank = nn(member.astype(BF16), before)
    local = index - jnp.sum(jnp.where(mine, group, 0), axis=0, keepdims=True) * TOK
    keys = jnp.where(mine, rank.astype(jnp.int32), -1)
    slow[...] = low_hot(keys)
    for g in range(4):
        shigh[g] = high_hot(keys, g)
    own_rank = jnp.max(keys, axis=0, keepdims=True)
    by_rank = pick(iota((128, TOK), 0) == own_rank).astype(BF16)
    part = iota((N_DP, 8, TOK), 1)
    high_bits = jnp.where(mine, (local >> 4) + 1, 0).astype(F32)
    low_bits = jnp.where(mine, local & 15, 0).astype(F32)
    marks = jnp.where(part == 6, high_bits[:, None, :], jnp.where(part == 7, low_bits[:, None, :], 0.0))
    extra = nt(marks.reshape(N_DP * 8, TOK).astype(BF16), by_rank)

    loads[1].wait()
    loads[2].wait()
    back_t = nt(adapter_ref[...], prompt_ref[...]).astype(BF16)
    send[0] = pack(slow, shigh, back_t, extra)

    def route(which):
        def step(k, carry):
            to = lax.rem(d + k, N_DP)
            rcopy(
                send.at[which, to], got.at[which, d],
                route_ss.at[which, k], route_rs.at[which, k], at(to, f),
            ).start()
            return carry

        lax.fori_loop(1, N_DP, step, 0)
        got[which, pl.ds(d, 1)] = send[which, pl.ds(d, 1)]

    def routed(which):
        def step(k, carry):
            come = lax.rem(d + N_DP - k, N_DP)
            rcopy(
                got.at[which, come], got.at[which, come],
                route_ss.at[which, k], route_rs.at[which, k], at(come, f),
            ).wait_recv()
            return carry

        lax.fori_loop(1, N_DP, step, 0)

    def route_sent(which):
        def step(k, carry):
            to = lax.rem(d + k, N_DP)
            rcopy(
                send.at[which, to], got.at[which, d],
                route_ss.at[which, k], route_rs.at[which, k], at(to, f),
            ).wait_send()
            return carry

        lax.fori_loop(1, N_DP, step, 0)

    route(0)
    frames_ag.relay()

    loads[3].wait()
    pad8 = jnp.zeros((CH, 8), BF16)
    for o in range(N_DP):
        lines = [weight_ref[k, :, TAPC * o : TAPC * o + TAPC] for k in (2, 1, 0)]
        weight_t[:, 128 * o : 128 * o + 128] = jnp.concatenate(lines + [pad8], axis=1)

    frames_ag.share()

    for o in range(N_DP):
        columns = prompt_ref[:, ECOL * o : ECOL * o + ECOL]
        prompt_pad[:, 128 * o : 128 * o + 128] = jnp.concatenate(
            [columns, jnp.zeros((TOK, 128 - ECOL), BF16)], axis=1
        )

    lane = iota((1, TOK), 1)
    inside = jnp.ones((1, TOK), F32)
    start = jnp.int32(0)
    for k in range(6):
        inside = jnp.where(lane == start, 0.0, inside)
        start = start + clips_ref[0, k]

    frames_ag.last()

    def weight_out(k, carry):
        to = lax.rem(f + k, N_FSDP)
        rcopy(
            weight_t.at[:, pl.ds(pl.multiple_of(to * 512, 512), 512)], weight_in.at[f],
            w_ss.at[k], w_rs.at[k], at(d, to),
        ).start()
        return carry

    lax.fori_loop(1, N_FSDP, weight_out, 0)
    weight_in[pl.ds(f, 1)] = weight_t[:, pl.ds(pl.multiple_of(f * 512, 512), 512)][None]

    live = pick(iota((48, TOK), 0) < TAPC) * inside

    def shift_in(o, carry):
        lines = xbuf[pl.ds(o, 1), pl.ds(0, 48), :][0].astype(F32)
        xbuf[pl.ds(o, 1), pl.ds(80, 48), :] = (pltpu.roll(lines, 1, 1) * live).astype(BF16)[None]
        return carry

    lax.fori_loop(0, N_DP, shift_in, 0)

    bias = bias_ref[...].astype(F32).reshape(1, CH)
    bias = jnp.sum(jnp.where(iota((CH, CH), 0) == iota((CH, CH), 1), bias, 0.0), axis=1, keepdims=True)
    preact = nn(weight_t[...], xbuf[...].reshape(N_DP * 128, TOK)) + bias
    cumul = 0.5 * (1.0 + lax.erf(preact * (1.0 / math.sqrt(2.0))))
    hidden_t = (preact * cumul).astype(BF16)
    slope = cumul + preact * jnp.exp(-0.5 * preact * preact) * (1.0 / math.sqrt(2.0 * math.pi))

    routed(0)
    tags = got[0, :, CAP:, :].astype(F32)
    numbers = (tags[:, 6, :] - 1.0) * 16.0 + tags[:, 7, :]

    def token_of(rows, first, most):
        spot = iota((N_DP, rows, 128), 1)
        match = (iota((N_DP, rows, 128), 2) == spot + first) & (spot < most)
        picked = jnp.sum(jnp.where(match, numbers[:, None, :], 0.0), axis=2, keepdims=True)
        ok = iota((N_DP, rows, 1), 1) < most
        return jnp.where(ok, picked, -1.0)

    def token_hot(rows, first, most):
        token = iota((N_DP, rows, TOK), 2).astype(F32)
        return pick(token_of(rows, first, most) == token).reshape(N_DP * rows, TOK).astype(BF16)

    dlow[...] = token_hot(CAP, 0, CAP)
    for g in range(4):
        dhigh[g] = token_hot(8, 6 * g, 6)
    send[1] = pack(dlow, dhigh, hidden_t)
    route(1)

    slope_t = (unpack(dlow, dhigh, got[0]) * slope).astype(BF16)
    slope_all[pl.ds(f, 1)] = slope_t[None]
    slope_ag = Gather(
        1,
        slope_all.at[f],
        lambda g: slope_all.at[g],
        lambda g, h: slope_all.at[g, pl.ds(80 * h, 80), :],
    )
    slope_ag.first()

    xr, xl, xo = lax.rem(x + 1, NX), lax.rem(x + NX - 1, NX), lax.rem(x + 2, NX)
    to_right, to_left = at(xr * NZ + z, f), at(xl * NZ + z, f)

    def halves(which, owner, h):
        return parts.at[which, pl.ds(owner * NZ + 4 * h, 4)]

    def rs_send(which, src, k, dev):
        go(src, rs_in.at[which, k], rs_ss.at[which, k], rs_rs.at[which, k], dev)

    def rs_wait(which, k):
        arrived(rs_in.at[which, k], rs_ss.at[which, k], rs_rs.at[which, k])

    def rs_first(which):
        rs_send(which, halves(which, xo, 0), 0, to_right)
        rs_send(which, halves(which, xo, 1), 1, to_left)
        rs_send(which, halves(which, xr, 1), 2, to_right)
        rs_send(which, halves(which, xl, 0), 3, to_left)

    def rs_second(which):
        rs_wait(which, 0)
        rs_out[which, 0] = (halves(which, xr, 0)[...].astype(F32) + rs_in[which, 0].astype(F32)).astype(BF16)
        rs_send(which, rs_out.at[which, 0], 4, to_right)
        rs_wait(which, 1)
        rs_out[which, 1] = (halves(which, xl, 1)[...].astype(F32) + rs_in[which, 1].astype(F32)).astype(BF16)
        rs_send(which, rs_out.at[which, 1], 5, to_left)

    def rs_third(which):
        for k in (2, 3, 4, 5):
            rs_wait(which, k)
        for h, (one, two) in enumerate(((4, 3), (5, 2))):
            total = halves(which, x, h)[...].astype(F32) + rs_in[which, one].astype(F32)
            total = total + rs_in[which, two].astype(F32)
            totals[which, pl.ds(4 * h, 4)] = total
            zsend[which, pl.ds(4 * h, 4)] = total.astype(BF16)

        def step(k, carry):
            to = lax.rem(z + k, NZ)
            rcopy(
                zsend.at[which, to], zgot.at[which, k],
                z_ss.at[which, k], z_rs.at[which, k], at(x * NZ + to, f),
            ).start()
            return carry

        lax.fori_loop(1, NZ, step, 0)

    def rs_last(which):
        total = totals[which, pl.ds(z, 1)][0]
        for k in range(1, NZ):
            arrived(zgot.at[which, k], z_ss.at[which, k], z_rs.at[which, k])
            total = total + zgot[which, k].astype(F32)
        return total * GRAD_SCALE

    def conv_part(o, carry):
        block = xbuf[pl.ds(o, 1)][0]
        parts[0, pl.ds(o, 1)] = nt(slope_all[pl.ds(f, 1)][0], block).astype(BF16)[None]
        return carry

    lax.fori_loop(0, N_DP, conv_part, 0)
    rs_first(0)
    slope_ag.relay()

    routed(1)
    hidden_pos = unpack(slow, shigh, got[1]).astype(BF16)
    for o in range(N_DP):
        parts[1, o] = nn(hidden_pos, prompt_pad[:, 128 * o : 128 * o + 128]).astype(BF16)
    rs_first(1)
    slope_ag.share()
    rs_second(0)

    def weight_come(k, carry):
        come = lax.rem(f + N_FSDP - k, N_FSDP)
        rcopy(
            weight_in.at[come], weight_in.at[come], w_ss.at[k], w_rs.at[k], at(d, come)
        ).wait_recv()
        return carry

    lax.fori_loop(1, N_FSDP, weight_come, 0)
    for g in range(N_FSDP):
        weight_own[:, CH * g : CH * g + CH] = weight_in[g].T
    rs_second(1)
    slope_ag.last()
    grads = nn(weight_own[...], slope_all[...].reshape(N_FSDP * CH, TOK))
    odd, even = [], []
    for q in range(4):
        lines = grads[128 * q : 128 * q + 128]
        odd.append(lines[:TAPC] + pltpu.roll(lines[2 * TAPC : 3 * TAPC] * inside, TOK - 1, 1))
        even.append(lines[TAPC : 2 * TAPC])
    odd = jnp.concatenate(odd, axis=0).astype(BF16)
    even = jnp.concatenate(even, axis=0).astype(BF16)
    for b in range(3):
        both = jnp.concatenate(
            [odd[:, 128 * b : 128 * b + 128], even[:, 128 * b : 128 * b + 128]], axis=1
        )
        hidden_ref[:, 256 * b : 256 * b + 256] = nt(both, halving[...]).astype(BF16)

    rs_third(0)
    rs_third(1)
    sums_ref[0] = rs_last(0)
    sums_ref[1] = rs_last(1)

    for copy in pending:
        copy.wait_send()
    route_sent(0)
    route_sent(1)

    def weight_sent(k, carry):
        to = lax.rem(f + k, N_FSDP)
        rcopy(
            weight_t.at[:, pl.ds(pl.multiple_of(to * 512, 512), 512)], weight_in.at[f],
            w_ss.at[k], w_rs.at[k], at(d, to),
        ).wait_send()
        return carry

    lax.fori_loop(1, N_FSDP, weight_sent, 0)

    def z_sent(k, carry):
        to = lax.rem(z + k, NZ)
        for which in range(2):
            rcopy(
                zsend.at[which, to], zgot.at[which, k],
                z_ss.at[which, k], z_rs.at[which, k], at(x * NZ + to, f),
            ).wait_send()
        return carry

    lax.fori_loop(1, NZ, z_sent, 0)


def finish(hidden_in, sums_ref, hidden_ref, gadapter_ref, gconv_ref):
    hidden_ref[...] = hidden_in[...]
    conv = sums_ref[0].T
    gconv_ref[0] = conv[2 * TAPC : 3 * TAPC]
    gconv_ref[1] = conv[TAPC : 2 * TAPC]
    gconv_ref[2] = conv[:TAPC]
    gadapter_ref[...] = sums_ref[1][:, :ECOL]


def body(
    hidden_frames, conv_weight, conv_bias, adapter_weight, prompt_grad, token_index, clip_tokens
):
    vmem = pl.BlockSpec(memory_space=pltpu.VMEM)
    smem = pl.BlockSpec(memory_space=pltpu.SMEM)
    hbm = pl.BlockSpec(memory_space=pl.ANY)
    dma = pltpu.SemaphoreType.DMA
    hidden, sums = pl.pallas_call(
        kernel,
        out_shape=(
            jax.ShapeDtypeStruct((CH, 2 * TOK), BF16),
            jax.ShapeDtypeStruct((2, CH, 128), F32),
        ),
        in_specs=[hbm, hbm, vmem, hbm, hbm, vmem, smem],
        out_specs=(vmem, vmem),
        scratch_shapes=[
            pltpu.VMEM((CH, 2 * TOK), BF16),
            pltpu.VMEM((3, CH, N_FSDP * CH), BF16),
            pltpu.VMEM((CH, WIDTH), BF16),
            pltpu.VMEM((TOK, WIDTH), BF16),
            dma((4,)),
            pltpu.VMEM((256, 256), BF16),
            pltpu.VMEM((TOK, N_DP * EPAD), BF16),
            pltpu.VMEM((CH, N_DP * 128), BF16),
            pltpu.VMEM((N_FSDP, CH, 512), BF16),
            pltpu.VMEM((512, N_FSDP * CH), BF16),
            pltpu.VMEM((4, 80, TOK), BF16),
            pltpu.VMEM((N_DP, 128, TOK), BF16),
            pltpu.VMEM((N_DP * CAP, TOK), BF16),
            pltpu.VMEM((4, N_DP * 8, TOK), BF16),
            pltpu.VMEM((N_DP * CAP, TOK), BF16),
            pltpu.VMEM((4, N_DP * 8, TOK), BF16),
            pltpu.VMEM((2, N_DP, 32, 128), BF16),
            pltpu.VMEM((2, N_DP, 32, 128), BF16),
            pltpu.VMEM((N_FSDP, CH, TOK), BF16),
            pltpu.VMEM((2, N_DP, CH, 128), BF16),
            pltpu.VMEM((2, 6, 4, CH, 128), BF16),
            pltpu.VMEM((2, 2, 4, CH, 128), BF16),
            pltpu.VMEM((2, NZ, CH, 128), BF16),
            pltpu.VMEM((2, NZ, CH, 128), BF16),
            pltpu.VMEM((2, NZ, CH, 128), F32),
            dma((2, N_DP)), dma((2, N_DP)),
            dma((2, 9)), dma((2, 9)),
            dma((N_FSDP,)), dma((N_FSDP,)),
            dma((2, 6)), dma((2, 6)),
            dma((2, NZ)), dma((2, NZ)),
        ],
        compiler_params=pltpu.CompilerParams(
            collective_id=0, has_side_effects=True, vmem_limit_bytes=56 * 1024 * 1024
        ),
    )(
        hidden_frames.T,
        jnp.swapaxes(conv_weight, 1, 2),
        conv_bias,
        adapter_weight,
        prompt_grad,
        token_index,
        clip_tokens,
    )
    hidden, gadapter, gconv = pl.pallas_call(
        finish,
        out_shape=(
            jax.ShapeDtypeStruct((CH, 2 * TOK), BF16),
            jax.ShapeDtypeStruct((CH, ECOL), F32),
            jax.ShapeDtypeStruct((3, TAPC, CH), F32),
        ),
        in_specs=[vmem, vmem],
        out_specs=(vmem, vmem, vmem),
    )(hidden, sums)
    return (hidden.T, gadapter, gconv)


def solution(mesh):
    placed = (
        P("dp", "fsdp"),
        P(None, None, "fsdp"),
        P("fsdp"),
        P("fsdp", None),
        P("dp", None),
        P("dp"),
        P("dp", None),
    )
    return jax.shard_map(
        body,
        mesh=mesh,
        in_specs=placed,
        out_specs=(P("dp", "fsdp"), P("fsdp", "dp"), P(None, "dp", "fsdp")),
        check_vma=False,
    )
```

```python
import math

import jax
import jax.numpy as jnp
from jax import lax
from jax.experimental import pallas as pl
from jax.experimental.pallas import tpu as pltpu
from jax.sharding import PartitionSpec as P

MESH = pl.DeviceIdType.MESH
F32 = jnp.float32
BF16 = jnp.bfloat16

NX, NZ, NY = 4, 8, 4
N_DP, N_FSDP = NX * NZ, 2 * NY
TOK = 384
CH = 160
WIDTH = 3584
CAP = 24
LOW = 128
ECOL, EPAD = WIDTH // N_DP, 128
TAPC = 40
GRAD_SCALE = 1.0 / math.sqrt(TOK * N_DP)


def nn(left, right):
    return lax.dot_general(left, right, (((1,), (0,)), ((), ())), preferred_element_type=F32)


def nt(left, right):
    return lax.dot_general(left, right, (((1,), (1,)), ((), ())), preferred_element_type=F32)


def iota(shape, dim):
    return lax.broadcasted_iota(jnp.int32, shape, dim)


def pick(cond):
    return jnp.where(cond, 1.0, 0.0).astype(F32)


def low_hot(keys):
    rows = iota((N_DP, CAP, TOK), 1)
    return pick(keys[:, None, :] == rows).reshape(N_DP * CAP, TOK).astype(BF16)


def high_hot(keys, group):
    rows = iota((N_DP, 8, TOK), 1)
    hit = (keys[:, None, :] == rows + 6 * group) & (rows < 6)
    return pick(hit).reshape(N_DP * 8, TOK).astype(BF16)


def pack(low_ref, high_ref, rows_t, extra=None):
    low = nt(low_ref[...], rows_t[:LOW])
    tail = rows_t[LOW:]
    zero = jnp.zeros((CH - LOW, TOK), BF16)
    high = extra
    for group in range(4):
        placed = jnp.concatenate([tail if g == group else zero for g in range(4)], axis=0)
        part = nt(high_ref[group], placed)
        high = part if high is None else high + part
    slabs = jnp.concatenate([low.reshape(N_DP, CAP, 128), high.reshape(N_DP, 8, 128)], axis=1)
    return slabs.astype(BF16)


def unpack(low_ref, high_ref, got):
    got = got.astype(F32)
    low = got[:, :CAP, :].reshape(N_DP * CAP, 128).T.astype(BF16)
    high = got[:, CAP:, :].reshape(N_DP * 8, 128).T.astype(BF16)
    low = nn(low, low_ref[...])
    tail = None
    for group in range(4):
        part = nn(high[32 * group : 32 * group + 32], high_ref[group])
        tail = part if tail is None else tail + part
    return jnp.concatenate([low, tail], axis=0)


def kernel(
    frames_hbm, weight_hbm, bias_ref, adapter_hbm, prompt_hbm, index_ref, clips_ref,
    hidden_ref, sums_ref,
    frames_ref, weight_ref, adapter_ref, prompt_ref, in_sem, halving,
    preact_ref, back_ref, prompt_pad, weight_t, weight_in, weight_own, xown, xbuf,
    slow, shigh, dlow, dhigh, send, got, slope_all,
    parts, rs_in, rs_out, zsend, zgot, totals,
    route_ss, route_rs, ag_ss, ag_rs, w_ss, w_rs, rs_ss, rs_rs, z_ss, z_rs,
):
    d = lax.axis_index("dp")
    f = lax.axis_index("fsdp")
    x, z = d // NZ, lax.rem(d, NZ)
    y, c = f // 2, lax.rem(f, 2)
    pending = []
    loads = [
        pltpu.make_async_copy(src, dst, in_sem.at[k])
        for k, (src, dst) in enumerate(
            (
                (frames_hbm, frames_ref),
                (adapter_hbm, adapter_ref),
                (prompt_hbm, prompt_ref),
                (weight_hbm, weight_ref),
            )
        )
    ]
    for load in loads:
        load.start()

    def at(dp, fs):
        return {"dp": dp, "fsdp": fs}

    def rcopy(src, dst, ssem, rsem, dev):
        return pltpu.make_async_remote_copy(
            src_ref=src, dst_ref=dst, send_sem=ssem, recv_sem=rsem,
            device_id=dev, device_id_type=MESH,
        )

    def go(src, dst, ssem, rsem, dev):
        copy = rcopy(src, dst, ssem, rsem, dev)
        copy.start()
        pending.append(copy)

    def arrived(dst, ssem, rsem):
        rcopy(dst, dst, ssem, rsem, at(d, f)).wait_recv()

    barrier = pltpu.get_barrier_semaphore()

    def greet_dp(k, carry):
        pl.semaphore_signal(
            barrier, inc=1, device_id=at(lax.rem(d + k, N_DP), f), device_id_type=MESH
        )
        return carry

    def greet_fsdp(k, carry):
        pl.semaphore_signal(
            barrier, inc=1, device_id=at(d, lax.rem(f + k, N_FSDP)), device_id_type=MESH
        )
        return carry

    lax.fori_loop(1, N_DP, greet_dp, 0)
    lax.fori_loop(1, N_FSDP, greet_fsdp, 0)

    row = iota((256, 256), 0)
    col = iota((256, 256), 1)
    halving[...] = pick(row == jnp.where(col < 128, 2 * col + 1, 2 * (col - 128))).astype(BF16)
    loads[0].wait()
    for b in range(3):
        lines = nn(frames_ref[:, 256 * b : 256 * b + 256], halving[...])
        for q in range(4):
            quarter = lines[TAPC * q : TAPC * q + TAPC]
            xown[q, :, 128 * b : 128 * b + 128] = jnp.concatenate(
                [quarter[:, :128], quarter[:, 128:]], axis=0
            ).astype(BF16)

    pl.semaphore_wait(barrier, N_DP - 1 + N_FSDP - 1)

    yr, yl, yo = lax.rem(y + 1, NY), lax.rem(y + NY - 1, NY), lax.rem(y + 2, NY)
    mate = at(d, y * 2 + 1 - c)

    class Gather:
        def __init__(self, which, own, block):
            self.ss, self.rs = ag_ss.at[which], ag_rs.at[which]
            self.own, self.block = own, block
            self.order = (yl, yr, yo)

        def send(self, src, dst, k, dev):
            go(src, dst, self.ss.at[k], self.rs.at[k], dev)

        def first(self):
            here = self.block(f)
            for k, to in enumerate((yr, yl, yo)):
                self.send(self.own, here, k, at(d, to * 2 + c))
            self.send(self.own, here, 3, mate)

        def forward(self, k):
            block = self.block(self.order[k] * 2 + c)
            arrived(block, self.ss.at[k], self.rs.at[k])
            self.send(block, block, 4 + k, mate)

        def from_mate(self, k):
            come = y if k == 3 else self.order[k - 4]
            arrived(self.block(come * 2 + 1 - c), self.ss.at[k], self.rs.at[k])

    frames_ag = Gather(0, xown, lambda g: xbuf.at[pl.ds(4 * g, 4), pl.ds(0, 80), :])
    frames_ag.first()
    xbuf[pl.ds(4 * f, 4), pl.ds(0, 80), :] = xown[...]

    index = index_ref[...].reshape(1, TOK)
    group = iota((N_DP, TOK), 0)
    mine = (index >= group * TOK) & (index < (group + 1) * TOK)
    member = pick(mine)
    before = pick(iota((TOK, TOK), 0) < iota((TOK, TOK), 1)).astype(BF16)
    rank = nn(member.astype(BF16), before)
    local = index - jnp.sum(jnp.where(mine, group, 0), axis=0, keepdims=True) * TOK
    keys = jnp.where(mine, rank.astype(jnp.int32), -1)
    slow[...] = low_hot(keys)
    for g in range(4):
        shigh[g] = high_hot(keys, g)
    own_rank = jnp.max(keys, axis=0, keepdims=True)
    by_rank = pick(iota((128, TOK), 0) == own_rank).astype(BF16)
    part = iota((N_DP, 8, TOK), 1)
    high_bits = jnp.where(mine, (local >> 4) + 1, 0).astype(F32)
    low_bits = jnp.where(mine, local & 15, 0).astype(F32)
    marks = jnp.where(part == 6, high_bits[:, None, :], jnp.where(part == 7, low_bits[:, None, :], 0.0))
    extra = nt(marks.reshape(N_DP * 8, TOK).astype(BF16), by_rank)

    loads[1].wait()
    loads[2].wait()
    back_t = nt(adapter_ref[...], prompt_ref[...]).astype(BF16)
    send[0] = pack(slow, shigh, back_t, extra)

    def route(which):
        def step(k, carry):
            to = lax.rem(d + k, N_DP)
            rcopy(
                send.at[which, to], got.at[which, d],
                route_ss.at[which, k], route_rs.at[which, k], at(to, f),
            ).start()
            return carry

        lax.fori_loop(1, N_DP, step, 0)
        got[which, pl.ds(d, 1)] = send[which, pl.ds(d, 1)]

    def routed(which):
        def step(k, carry):
            come = lax.rem(d + N_DP - k, N_DP)
            rcopy(
                got.at[which, come], got.at[which, come],
                route_ss.at[which, k], route_rs.at[which, k], at(come, f),
            ).wait_recv()
            return carry

        lax.fori_loop(1, N_DP, step, 0)

    def route_sent(which):
        def step(k, carry):
            to = lax.rem(d + k, N_DP)
            rcopy(
                send.at[which, to], got.at[which, d],
                route_ss.at[which, k], route_rs.at[which, k], at(to, f),
            ).wait_send()
            return carry

        lax.fori_loop(1, N_DP, step, 0)

    route(0)

    loads[3].wait()
    pad8 = jnp.zeros((CH, 8), BF16)
    for o in range(N_DP):
        lines = [weight_ref[k, :, TAPC * o : TAPC * o + TAPC] for k in (2, 1, 0)]
        weight_t[:, 128 * o : 128 * o + 128] = jnp.concatenate(lines + [pad8], axis=1)

    lane = iota((1, TOK), 1)
    inside = jnp.ones((1, TOK), F32)
    start = jnp.int32(0)
    for k in range(6):
        inside = jnp.where(lane == start, 0.0, inside)
        start = start + clips_ref[0, k]
    live = pick(iota((48, TOK), 0) < TAPC) * inside

    bias = bias_ref[...].astype(F32).reshape(1, CH)
    bias = jnp.sum(jnp.where(iota((CH, CH), 0) == iota((CH, CH), 1), bias, 0.0), axis=1, keepdims=True)
    preact_ref[...] = jnp.broadcast_to(bias, (CH, TOK))

    def preact_block(g):
        for q in range(4):
            lines = xbuf[pl.ds(4 * g + q, 1), pl.ds(0, 48), :][0].astype(F32)
            early = (pltpu.roll(lines, 1, 1) * live).astype(BF16)
            xbuf[pl.ds(4 * g + q, 1), pl.ds(80, 48), :] = early[None]
        block = xbuf[pl.ds(4 * g, 4)].reshape(512, TOK)
        preact_ref[...] += nn(weight_t[:, pl.ds(pl.multiple_of(g * 512, 512), 512)], block)

    preact_block(f)
    for k in range(2):
        frames_ag.forward(k)
    frames_ag.from_mate(3)
    preact_block(y * 2 + 1 - c)

    for o in range(N_DP // 2):
        columns = prompt_ref[:, ECOL * o : ECOL * o + ECOL]
        prompt_pad[:, 128 * o : 128 * o + 128] = jnp.concatenate(
            [columns, jnp.zeros((TOK, 128 - ECOL), BF16)], axis=1
        )

    frames_ag.forward(2)

    def weight_out(k, carry):
        to = lax.rem(f + k, N_FSDP)
        rcopy(
            weight_t.at[:, pl.ds(pl.multiple_of(to * 512, 512), 512)], weight_in.at[f],
            w_ss.at[k], w_rs.at[k], at(d, to),
        ).start()
        return carry

    lax.fori_loop(1, N_FSDP, weight_out, 0)
    weight_in[pl.ds(f, 1)] = weight_t[:, pl.ds(pl.multiple_of(f * 512, 512), 512)][None]

    for k in range(3):
        preact_block(frames_ag.order[k] * 2 + c)

    routed(0)
    tags = got[0, :, CAP:, :].astype(F32)
    numbers = (tags[:, 6, :] - 1.0) * 16.0 + tags[:, 7, :]

    def token_of(rows, first, most):
        spot = iota((N_DP, rows, 128), 1)
        match = (iota((N_DP, rows, 128), 2) == spot + first) & (spot < most)
        picked = jnp.sum(jnp.where(match, numbers[:, None, :], 0.0), axis=2, keepdims=True)
        ok = iota((N_DP, rows, 1), 1) < most
        return jnp.where(ok, picked, -1.0)

    def token_hot(rows, first, most):
        token = iota((N_DP, rows, TOK), 2).astype(F32)
        return pick(token_of(rows, first, most) == token).reshape(N_DP * rows, TOK).astype(BF16)

    dlow[...] = token_hot(CAP, 0, CAP)
    for g in range(4):
        dhigh[g] = token_hot(8, 6 * g, 6)
    back_ref[...] = unpack(dlow, dhigh, got[0])

    for k in range(3):
        frames_ag.from_mate(4 + k)
        preact_block(frames_ag.order[k] * 2 + 1 - c)

    preact = preact_ref[...]
    cumul = 0.5 * (1.0 + lax.erf(preact * (1.0 / math.sqrt(2.0))))
    hidden_t = (preact * cumul).astype(BF16)
    send[1] = pack(dlow, dhigh, hidden_t)
    route(1)

    slope = cumul + preact * jnp.exp(-0.5 * preact * preact) * (1.0 / math.sqrt(2.0 * math.pi))
    slope_t = (back_ref[...] * slope).astype(BF16)
    slope_all[pl.ds(f, 1)] = slope_t[None]
    slope_ag = Gather(1, slope_all.at[f], lambda g: slope_all.at[g])
    slope_ag.first()

    xr, xl, xo = lax.rem(x + 1, NX), lax.rem(x + NX - 1, NX), lax.rem(x + 2, NX)
    to_right, to_left = at(xr * NZ + z, f), at(xl * NZ + z, f)

    def halves(which, owner, h):
        return parts.at[which, pl.ds(owner * NZ + 4 * h, 4)]

    def rs_send(which, src, k, dev):
        go(src, rs_in.at[which, k], rs_ss.at[which, k], rs_rs.at[which, k], dev)

    def rs_wait(which, k):
        arrived(rs_in.at[which, k], rs_ss.at[which, k], rs_rs.at[which, k])

    def rs_first(which, part):
        part(xo, 0)
        rs_send(which, halves(which, xo, 0), 0, to_right)
        part(xo, 1)
        rs_send(which, halves(which, xo, 1), 1, to_left)
        part(xr, 1)
        rs_send(which, halves(which, xr, 1), 2, to_right)
        part(xl, 0)
        rs_send(which, halves(which, xl, 0), 3, to_left)
        part(xr, 0)
        part(xl, 1)

    def rs_second(which):
        rs_wait(which, 0)
        rs_out[which, 0] = (halves(which, xr, 0)[...].astype(F32) + rs_in[which, 0].astype(F32)).astype(BF16)
        rs_send(which, rs_out.at[which, 0], 4, to_right)
        rs_wait(which, 1)
        rs_out[which, 1] = (halves(which, xl, 1)[...].astype(F32) + rs_in[which, 1].astype(F32)).astype(BF16)
        rs_send(which, rs_out.at[which, 1], 5, to_left)

    def rs_third(which):
        for k in (2, 3, 4, 5):
            rs_wait(which, k)
        for h, (one, two) in enumerate(((4, 3), (5, 2))):
            total = halves(which, x, h)[...].astype(F32) + rs_in[which, one].astype(F32)
            total = total + rs_in[which, two].astype(F32)
            totals[which, pl.ds(4 * h, 4)] = total
            zsend[which, pl.ds(4 * h, 4)] = total.astype(BF16)

        def step(k, carry):
            to = lax.rem(z + k, NZ)
            rcopy(
                zsend.at[which, to], zgot.at[which, k],
                z_ss.at[which, k], z_rs.at[which, k], at(x * NZ + to, f),
            ).start()
            return carry

        lax.fori_loop(1, NZ, step, 0)

    def rs_last(which):
        total = totals[which, pl.ds(z, 1)][0]
        for k in range(1, NZ):
            arrived(zgot.at[which, k], z_ss.at[which, k], z_rs.at[which, k])
            total = total + zgot[which, k].astype(F32)
        return total * GRAD_SCALE

    def store_parts(which, g, block):
        for q in range(4):
            parts[which, pl.ds(4 * g + q, 1)] = block[:, 128 * q : 128 * q + 128].astype(BF16)[None]

    def conv_part(owner, h):
        g = 2 * owner + h
        store_parts(0, g, nt(slope_t, xbuf[pl.ds(4 * g, 4)].reshape(512, TOK)))

    def adapter_part(owner, h):
        g = 2 * owner + h
        store_parts(1, g, nn(hidden_pos, prompt_pad[:, pl.ds(pl.multiple_of(g * 512, 512), 512)]))

    rs_first(0, conv_part)
    for o in range(N_DP // 2, N_DP):
        columns = prompt_ref[:, ECOL * o : ECOL * o + ECOL]
        prompt_pad[:, 128 * o : 128 * o + 128] = jnp.concatenate(
            [columns, jnp.zeros((TOK, 128 - ECOL), BF16)], axis=1
        )
    conv_part(x, 0)
    conv_part(x, 1)

    routed(1)
    hidden_pos = unpack(slow, shigh, got[1]).astype(BF16)
    rs_first(1, adapter_part)
    rs_second(0)
    for k in range(3):
        slope_ag.forward(k)
    adapter_part(x, 0)
    adapter_part(x, 1)
    rs_third(0)
    rs_second(1)

    def weight_come(k, carry):
        come = lax.rem(f + N_FSDP - k, N_FSDP)
        rcopy(
            weight_in.at[come], weight_in.at[come], w_ss.at[k], w_rs.at[k], at(d, come)
        ).wait_recv()
        return carry

    lax.fori_loop(1, N_FSDP, weight_come, 0)
    for g in range(N_FSDP):
        weight_own[:, CH * g : CH * g + CH] = weight_in[g].T
    rs_third(1)

    for k in range(3, 7):
        slope_ag.from_mate(k)
    grads = nn(weight_own[...], slope_all[...].reshape(N_FSDP * CH, TOK))
    odd, even = [], []
    for q in range(4):
        lines = grads[128 * q : 128 * q + 128]
        odd.append(lines[:TAPC] + pltpu.roll(lines[2 * TAPC : 3 * TAPC] * inside, TOK - 1, 1))
        even.append(lines[TAPC : 2 * TAPC])
    odd = jnp.concatenate(odd, axis=0).astype(BF16)
    even = jnp.concatenate(even, axis=0).astype(BF16)
    for b in range(3):
        both = jnp.concatenate(
            [odd[:, 128 * b : 128 * b + 128], even[:, 128 * b : 128 * b + 128]], axis=1
        )
        hidden_ref[:, 256 * b : 256 * b + 256] = nt(both, halving[...]).astype(BF16)

    sums_ref[0] = rs_last(0)
    sums_ref[1] = rs_last(1)

    for copy in pending:
        copy.wait_send()
    route_sent(0)
    route_sent(1)

    def weight_sent(k, carry):
        to = lax.rem(f + k, N_FSDP)
        rcopy(
            weight_t.at[:, pl.ds(pl.multiple_of(to * 512, 512), 512)], weight_in.at[f],
            w_ss.at[k], w_rs.at[k], at(d, to),
        ).wait_send()
        return carry

    lax.fori_loop(1, N_FSDP, weight_sent, 0)

    def z_sent(k, carry):
        to = lax.rem(z + k, NZ)
        for which in range(2):
            rcopy(
                zsend.at[which, to], zgot.at[which, k],
                z_ss.at[which, k], z_rs.at[which, k], at(x * NZ + to, f),
            ).wait_send()
        return carry

    lax.fori_loop(1, NZ, z_sent, 0)


def finish(hidden_in, sums_ref, hidden_ref, gadapter_ref, gconv_ref):
    hidden_ref[...] = hidden_in[...]
    conv = sums_ref[0].T
    gconv_ref[0] = conv[2 * TAPC : 3 * TAPC]
    gconv_ref[1] = conv[TAPC : 2 * TAPC]
    gconv_ref[2] = conv[:TAPC]
    gadapter_ref[...] = sums_ref[1][:, :ECOL]


def body(
    hidden_frames, conv_weight, conv_bias, adapter_weight, prompt_grad, token_index, clip_tokens
):
    vmem = pl.BlockSpec(memory_space=pltpu.VMEM)
    smem = pl.BlockSpec(memory_space=pltpu.SMEM)
    hbm = pl.BlockSpec(memory_space=pl.ANY)
    dma = pltpu.SemaphoreType.DMA
    hidden, sums = pl.pallas_call(
        kernel,
        out_shape=(
            jax.ShapeDtypeStruct((CH, 2 * TOK), BF16),
            jax.ShapeDtypeStruct((2, CH, 128), F32),
        ),
        in_specs=[hbm, hbm, vmem, hbm, hbm, vmem, smem],
        out_specs=(vmem, vmem),
        scratch_shapes=[
            pltpu.VMEM((CH, 2 * TOK), BF16),
            pltpu.VMEM((3, CH, N_FSDP * CH), BF16),
            pltpu.VMEM((CH, WIDTH), BF16),
            pltpu.VMEM((TOK, WIDTH), BF16),
            dma((4,)),
            pltpu.VMEM((256, 256), BF16),
            pltpu.VMEM((CH, TOK), F32),
            pltpu.VMEM((CH, TOK), F32),
            pltpu.VMEM((TOK, N_DP * EPAD), BF16),
            pltpu.VMEM((CH, N_DP * 128), BF16),
            pltpu.VMEM((N_FSDP, CH, 512), BF16),
            pltpu.VMEM((512, N_FSDP * CH), BF16),
            pltpu.VMEM((4, 80, TOK), BF16),
            pltpu.VMEM((N_DP, 128, TOK), BF16),
            pltpu.VMEM((N_DP * CAP, TOK), BF16),
            pltpu.VMEM((4, N_DP * 8, TOK), BF16),
            pltpu.VMEM((N_DP * CAP, TOK), BF16),
            pltpu.VMEM((4, N_DP * 8, TOK), BF16),
            pltpu.VMEM((2, N_DP, 32, 128), BF16),
            pltpu.VMEM((2, N_DP, 32, 128), BF16),
            pltpu.VMEM((N_FSDP, CH, TOK), BF16),
            pltpu.VMEM((2, N_DP, CH, 128), BF16),
            pltpu.VMEM((2, 6, 4, CH, 128), BF16),
            pltpu.VMEM((2, 2, 4, CH, 128), BF16),
            pltpu.VMEM((2, NZ, CH, 128), BF16),
            pltpu.VMEM((2, NZ, CH, 128), BF16),
            pltpu.VMEM((2, NZ, CH, 128), F32),
            dma((2, N_DP)), dma((2, N_DP)),
            dma((2, 7)), dma((2, 7)),
            dma((N_FSDP,)), dma((N_FSDP,)),
            dma((2, 6)), dma((2, 6)),
            dma((2, NZ)), dma((2, NZ)),
        ],
        compiler_params=pltpu.CompilerParams(
            collective_id=0, has_side_effects=True, vmem_limit_bytes=56 * 1024 * 1024
        ),
    )(
        hidden_frames.T,
        jnp.swapaxes(conv_weight, 1, 2),
        conv_bias,
        adapter_weight,
        prompt_grad,
        token_index,
        clip_tokens,
    )
    hidden, gadapter, gconv = pl.pallas_call(
        finish,
        out_shape=(
            jax.ShapeDtypeStruct((CH, 2 * TOK), BF16),
            jax.ShapeDtypeStruct((CH, ECOL), F32),
            jax.ShapeDtypeStruct((3, TAPC, CH), F32),
        ),
        in_specs=[vmem, vmem],
        out_specs=(vmem, vmem, vmem),
    )(hidden, sums)
    return (hidden.T, gadapter, gconv)


def solution(mesh):
    placed = (
        P("dp", "fsdp"),
        P(None, None, "fsdp"),
        P("fsdp"),
        P("fsdp", None),
        P("dp", None),
        P("dp"),
        P("dp", None),
    )
    return jax.shard_map(
        body,
        mesh=mesh,
        in_specs=placed,
        out_specs=(P("dp", "fsdp"), P("fsdp", "dp"), P(None, "dp", "fsdp")),
        check_vma=False,
    )
```

```python
import math

import jax
import jax.numpy as jnp
from jax import lax
from jax.experimental import pallas as pl
from jax.experimental.pallas import tpu as pltpu
from jax.sharding import PartitionSpec as P

MESH = pl.DeviceIdType.MESH
F32 = jnp.float32
BF16 = jnp.bfloat16

NX, NZ, NY = 4, 8, 4
N_DP, N_FSDP = NX * NZ, 2 * NY
TOK = 384
CH = 160
WIDTH = 3584
CAP = 24
LOW = 128
ECOL = WIDTH // N_DP
QUARTER = WIDTH // NX
TAPC = 40
GRAD_SCALE = 1.0 / math.sqrt(TOK * N_DP)


def nn(left, right):
    return lax.dot_general(left, right, (((1,), (0,)), ((), ())), preferred_element_type=F32)


def nt(left, right):
    return lax.dot_general(left, right, (((1,), (1,)), ((), ())), preferred_element_type=F32)


def iota(shape, dim):
    return lax.broadcasted_iota(jnp.int32, shape, dim)


def pick(cond):
    return jnp.where(cond, 1.0, 0.0).astype(F32)


def low_hot(keys):
    rows = iota((N_DP, CAP, TOK), 1)
    return pick(keys[:, None, :] == rows).reshape(N_DP * CAP, TOK).astype(BF16)


def high_hot(keys, group):
    rows = iota((N_DP, 8, TOK), 1)
    hit = (keys[:, None, :] == rows + 6 * group) & (rows < 6)
    return pick(hit).reshape(N_DP * 8, TOK).astype(BF16)


def pack(low_ref, high_ref, rows_t, extra=None):
    low = nt(low_ref[...], rows_t[:LOW])
    tail = rows_t[LOW:]
    zero = jnp.zeros((CH - LOW, TOK), BF16)
    high = extra
    for group in range(4):
        placed = jnp.concatenate([tail if g == group else zero for g in range(4)], axis=0)
        part = nt(high_ref[group], placed)
        high = part if high is None else high + part
    slabs = jnp.concatenate([low.reshape(N_DP, CAP, 128), high.reshape(N_DP, 8, 128)], axis=1)
    return slabs.astype(BF16)


def unpack(low_ref, high_ref, got):
    got = got.astype(F32)
    low = got[:, :CAP, :].reshape(N_DP * CAP, 128).T.astype(BF16)
    high = got[:, CAP:, :].reshape(N_DP * 8, 128).T.astype(BF16)
    low = nn(low, low_ref[...])
    tail = None
    for group in range(4):
        part = nn(high[32 * group : 32 * group + 32], high_ref[group])
        tail = part if tail is None else tail + part
    return jnp.concatenate([low, tail], axis=0)


def kernel(
    frames_hbm, weight_hbm, bias_ref, adapter_hbm, prompt_hbm, index_ref, clips_ref,
    hidden_ref, sums_ref,
    frames_all, weight_ref, adapter_ref, prompt_ref, in_sem, halving,
    preact_ref, back_ref, weight_t, weight_in, weight_own, xbuf,
    slow, shigh, dlow, dhigh, send, got, slope_all,
    columns_in, hidden_all, adapter_quarter, adapter_sum,
    parts, rs_in, rs_out, conv_sum, conv_send, conv_got, conv_relay,
    parts_got, parts_relay, parts_sum, parts_send, parts_last,
    adapter_send, adapter_got, adapter_relay,
    route_ss, route_rs, ag_ss, ag_rs, w_ss, w_rs, rs_ss, rs_rs, z_ss, z_rs, x_ss, x_rs,
):
    d = lax.axis_index("dp")
    f = lax.axis_index("fsdp")
    x, z = d // NZ, lax.rem(d, NZ)
    y, c = f // 2, lax.rem(f, 2)
    pending = []
    loads = [
        pltpu.make_async_copy(src, dst, in_sem.at[k])
        for k, (src, dst) in enumerate(
            (
                (frames_hbm, frames_all.at[f]),
                *(
                    (prompt_hbm.at[:, pl.ds(QUARTER * q, QUARTER)], prompt_ref.at[q])
                    for q in range(NX)
                ),
                (adapter_hbm, adapter_ref),
                (weight_hbm, weight_ref),
            )
        )
    ]
    for load in loads:
        load.start()

    def at(dp, fs):
        return {"dp": dp, "fsdp": fs}

    def rcopy(src, dst, ssem, rsem, dev):
        return pltpu.make_async_remote_copy(
            src_ref=src, dst_ref=dst, send_sem=ssem, recv_sem=rsem,
            device_id=dev, device_id_type=MESH,
        )

    def go(src, dst, ssem, rsem, dev):
        copy = rcopy(src, dst, ssem, rsem, dev)
        copy.start()
        pending.append(copy)

    def arrived(dst, ssem, rsem):
        rcopy(dst, dst, ssem, rsem, at(d, f)).wait_recv()

    barrier = pltpu.get_barrier_semaphore()

    def greet_dp(k, carry):
        pl.semaphore_signal(
            barrier, inc=1, device_id=at(lax.rem(d + k, N_DP), f), device_id_type=MESH
        )
        return carry

    def greet_fsdp(k, carry):
        pl.semaphore_signal(
            barrier, inc=1, device_id=at(d, lax.rem(f + k, N_FSDP)), device_id_type=MESH
        )
        return carry

    lax.fori_loop(1, N_DP, greet_dp, 0)
    lax.fori_loop(1, N_FSDP, greet_fsdp, 0)

    pl.semaphore_wait(barrier, N_DP - 1 + N_FSDP - 1)

    yr, yl, yo = lax.rem(y + 1, NY), lax.rem(y + NY - 1, NY), lax.rem(y + 2, NY)
    mate = at(d, y * 2 + 1 - c)

    class Gather:
        def __init__(self, which, own, buf):
            self.ss, self.rs = ag_ss.at[which], ag_rs.at[which]
            self.own, self.buf = own, buf

        def send(self, src, dst, k, dev):
            go(src, dst, self.ss.at[k], self.rs.at[k], dev)

        def half(self, g, h):
            return self.buf.at[g, pl.ds(80 * h, 80)]

        def come(self, dst, k):
            arrived(dst, self.ss.at[k], self.rs.at[k])

        def first(self):
            for h in range(2):
                for k, (to, part) in enumerate(((yr, h), (yl, 1 - h))):
                    src = self.own.at[pl.ds(80 * part, 80)]
                    self.send(src, self.half(f, part), 2 * k + part, at(d, to * 2 + c))
            self.send(self.own, self.buf.at[f], 6, mate)

        def relay(self):
            for k, (come, to) in enumerate(((yl, yr), (yr, yl))):
                block = self.half(come * 2 + c, k)
                self.come(block, 2 * k + k)
                self.send(block, block, 4 + k, at(d, to * 2 + c))

        def near(self):
            for k, come in enumerate((yl, yr)):
                self.come(self.half(come * 2 + c, 1 - k), 2 * k + 1 - k)
                block = self.buf.at[come * 2 + c]
                self.send(block, block, 7 + k, mate)

        def far(self):
            for h in range(2):
                block = self.half(yo * 2 + c, h)
                self.come(block, 4 + h)
                self.send(block, block, 9 + h, mate)

        def from_mate(self, k):
            o = 1 - c
            if k < 3:
                self.come(self.buf.at[(y, yl, yr)[k] * 2 + o], 6 + k)
            else:
                self.come(self.half(yo * 2 + o, 0), 9)
                self.come(self.half(yo * 2 + o, 1), 10)

    frames_ag = Gather(0, frames_hbm, frames_all)
    frames_ag.first()

    row = iota((256, 256), 0)
    col = iota((256, 256), 1)
    halving[...] = pick(row == jnp.where(col < 128, 2 * col + 1, 2 * (col - 128))).astype(BF16)

    index = index_ref[...].reshape(1, TOK)
    group = iota((N_DP, TOK), 0)
    mine = (index >= group * TOK) & (index < (group + 1) * TOK)
    member = pick(mine)
    before = pick(iota((TOK, TOK), 0) < iota((TOK, TOK), 1)).astype(BF16)
    rank = nn(member.astype(BF16), before)
    local = index - jnp.sum(jnp.where(mine, group, 0), axis=0, keepdims=True) * TOK
    keys = jnp.where(mine, rank.astype(jnp.int32), -1)
    slow[...] = low_hot(keys)
    for g in range(4):
        shigh[g] = high_hot(keys, g)
    own_rank = jnp.max(keys, axis=0, keepdims=True)
    by_rank = pick(iota((128, TOK), 0) == own_rank).astype(BF16)
    part = iota((N_DP, 8, TOK), 1)
    high_bits = jnp.where(mine, (local >> 4) + 1, 0).astype(F32)
    low_bits = jnp.where(mine, local & 15, 0).astype(F32)
    marks = jnp.where(part == 6, high_bits[:, None, :], jnp.where(part == 7, low_bits[:, None, :], 0.0))
    extra = nt(marks.reshape(N_DP * 8, TOK).astype(BF16), by_rank)

    for q in range(NX):
        loads[1 + q].wait()
    loads[5].wait()
    back_t = nt(adapter_ref[:, :QUARTER], prompt_ref[0])
    for q in range(1, NX):
        back_t = back_t + nt(adapter_ref[:, QUARTER * q : QUARTER * q + QUARTER], prompt_ref[q])
    back_t = back_t.astype(BF16)
    send[0] = pack(slow, shigh, back_t, extra)

    def route(which):
        def step(k, carry):
            to = lax.rem(d + k, N_DP)
            rcopy(
                send.at[which, to], got.at[which, d],
                route_ss.at[which, k], route_rs.at[which, k], at(to, f),
            ).start()
            return carry

        lax.fori_loop(1, N_DP, step, 0)
        got[which, pl.ds(d, 1)] = send[which, pl.ds(d, 1)]

    def routed(which):
        def step(k, carry):
            come = lax.rem(d + N_DP - k, N_DP)
            rcopy(
                got.at[which, come], got.at[which, come],
                route_ss.at[which, k], route_rs.at[which, k], at(come, f),
            ).wait_recv()
            return carry

        lax.fori_loop(1, N_DP, step, 0)

    def route_sent(which):
        def step(k, carry):
            to = lax.rem(d + k, N_DP)
            rcopy(
                send.at[which, to], got.at[which, d],
                route_ss.at[which, k], route_rs.at[which, k], at(to, f),
            ).wait_send()
            return carry

        lax.fori_loop(1, N_DP, step, 0)

    route(0)

    xr, xl, xo = lax.rem(x + 1, NX), lax.rem(x + NX - 1, NX), lax.rem(x + 2, NX)
    x_order = ((1, xr), (3, xl), (2, xo))
    half = pl.ds(pl.multiple_of(192 * c, 192), 192)
    other_half = pl.ds(pl.multiple_of(192 - 192 * c, 192), 192)
    for k, to in x_order:
        go(
            prompt_ref.at[to, half],
            columns_in.at[k, half],
            x_ss.at[0, k], x_rs.at[0, k], at(to * NZ + z, f),
        )

    loads[6].wait()
    pad8 = jnp.zeros((CH, 8), BF16)
    for o in range(N_DP):
        lines = [weight_ref[k, :, TAPC * o : TAPC * o + TAPC] for k in (2, 1, 0)]
        weight_t[:, 128 * o : 128 * o + 128] = jnp.concatenate(lines + [pad8], axis=1)

    lane = iota((1, TOK), 1)
    inside = jnp.ones((1, TOK), F32)
    start = jnp.int32(0)
    for k in range(6):
        inside = jnp.where(lane == start, 0.0, inside)
        start = start + clips_ref[0, k]
    pad_rows = jnp.zeros((8, TOK), F32)

    bias = bias_ref[...].astype(F32).reshape(1, CH)
    bias = jnp.sum(jnp.where(iota((CH, CH), 0) == iota((CH, CH), 1), bias, 0.0), axis=1, keepdims=True)
    preact_ref[...] = jnp.broadcast_to(bias, (CH, TOK))

    def preact_block(g):
        lines = [
            nn(frames_all[pl.ds(g, 1), :, 256 * b : 256 * b + 256][0], halving[...]) for b in range(3)
        ]
        odd = jnp.concatenate([part[:, :128] for part in lines], axis=1)
        even = jnp.concatenate([part[:, 128:] for part in lines], axis=1)
        early = pltpu.roll(odd, 1, 1) * inside
        blocks = []
        for q in range(4):
            rows = slice(TAPC * q, TAPC * q + TAPC)
            blocks += [odd[rows], even[rows], early[rows], pad_rows]
        block = jnp.concatenate(blocks, axis=0).astype(BF16)
        xbuf[pl.ds(4 * g, 4)] = block.reshape(4, 128, TOK)
        preact_ref[...] += nn(weight_t[:, pl.ds(pl.multiple_of(g * 512, 512), 512)], block)

    loads[0].wait()
    preact_block(f)
    frames_ag.relay()
    frames_ag.from_mate(0)
    preact_block(y * 2 + 1 - c)
    frames_ag.near()
    preact_block(yl * 2 + c)
    preact_block(yr * 2 + c)
    frames_ag.far()

    def weight_out(k, carry):
        to = lax.rem(f + k, N_FSDP)
        rcopy(
            weight_t.at[:, pl.ds(pl.multiple_of(to * 512, 512), 512)], weight_in.at[f],
            w_ss.at[k], w_rs.at[k], at(d, to),
        ).start()
        return carry

    lax.fori_loop(1, N_FSDP, weight_out, 0)
    weight_in[pl.ds(f, 1)] = weight_t[:, pl.ds(pl.multiple_of(f * 512, 512), 512)][None]

    preact_block(yo * 2 + c)

    routed(0)
    tags = got[0, :, CAP:, :].astype(F32)
    numbers = (tags[:, 6, :] - 1.0) * 16.0 + tags[:, 7, :]

    def token_of(rows, first, most):
        spot = iota((N_DP, rows, 128), 1)
        match = (iota((N_DP, rows, 128), 2) == spot + first) & (spot < most)
        picked = jnp.sum(jnp.where(match, numbers[:, None, :], 0.0), axis=2, keepdims=True)
        ok = iota((N_DP, rows, 1), 1) < most
        return jnp.where(ok, picked, -1.0)

    def token_hot(rows, first, most):
        token = iota((N_DP, rows, TOK), 2).astype(F32)
        return pick(token_of(rows, first, most) == token).reshape(N_DP * rows, TOK).astype(BF16)

    dlow[...] = token_hot(CAP, 0, CAP)
    for g in range(4):
        dhigh[g] = token_hot(8, 6 * g, 6)
    back_ref[...] = unpack(dlow, dhigh, got[0])

    for k, come in ((1, yl), (2, yr), (3, yo)):
        frames_ag.from_mate(k)
        preact_block(come * 2 + 1 - c)

    preact = preact_ref[...]
    cumul = 0.5 * (1.0 + lax.erf(preact * (1.0 / math.sqrt(2.0))))
    hidden_t = (preact * cumul).astype(BF16)
    send[1] = pack(dlow, dhigh, hidden_t)
    route(1)

    slope = cumul + preact * jnp.exp(-0.5 * preact * preact) * (1.0 / math.sqrt(2.0 * math.pi))
    slope_t = (back_ref[...] * slope).astype(BF16)
    slope_all[pl.ds(f, 1)] = slope_t[None]
    slope_ag = Gather(1, slope_all.at[f], slope_all)
    slope_ag.first()

    to_right, to_left = at(xr * NZ + z, f), at(xl * NZ + z, f)

    def halves(owner, h):
        return parts.at[owner, pl.ds(4 * h, 4), pl.ds(0, 80)]

    def rs_send(src, k, dev):
        go(src, rs_in.at[k], rs_ss.at[k], rs_rs.at[k], dev)

    def rs_wait(k):
        arrived(rs_in.at[k], rs_ss.at[k], rs_rs.at[k])

    def conv_part(owner, h):
        g = 2 * owner + h
        block = nt(slope_t, xbuf[pl.ds(4 * g, 4)].reshape(512, TOK))
        for q in range(4):
            parts[pl.ds(owner, 1), 4 * h + q] = block[:, 128 * q : 128 * q + 128].astype(BF16)[None]

    def rs_second():
        for k, owner, dev in ((0, xr, to_right), (1, xl, to_left)):
            rs_wait(k)
            total = halves(owner, k)[...].astype(F32) + rs_in[k].astype(F32)
            rs_out[k] = total.astype(BF16)
            rs_send(rs_out.at[k], 4 + k, dev)

    def rs_third():
        for k in (2, 3, 4, 5):
            rs_wait(k)
        for h, (one, two) in enumerate(((4, 3), (5, 2))):
            total = halves(x, h)[...].astype(F32) + rs_in[one].astype(F32)
            total = total + rs_in[two].astype(F32)
            conv_sum[pl.ds(4 * h, 4)] = total
            conv_send[pl.ds(4 * h, 4)] = total.astype(BF16)

    def z_at(offset):
        return lax.rem(z + NZ + offset, NZ)

    class ZSum:
        def __init__(self, which, chunk, value, dst, relay):
            self.ss, self.rs = z_ss.at[which], z_rs.at[which]
            self.chunk, self.value, self.dst, self.relayed = chunk, value, dst, relay

        def send(self, src, slot, to):
            go(src, self.dst.at[slot], self.ss.at[slot], self.rs.at[slot], at(x * NZ + z_at(to), f))

        def wait(self, slot):
            arrived(self.dst.at[slot], self.ss.at[slot], self.rs.at[slot])
            return self.dst[slot].astype(F32)

        def first(self):
            for slot, chunk, to in ((5, -4, -2), (6, -3, -1), (7, 3, 1), (1, 1, 1), (2, -1, -1)):
                self.send(self.chunk(z_at(chunk)), slot, to)

        def relay(self):
            total = self.value(z_at(-2)) + self.wait(5) + self.wait(6)
            self.relayed[0] = total.astype(BF16)
            self.send(self.relayed.at[0], 3, -2)
            self.relayed[1] = (self.value(z_at(2)) + self.wait(7)).astype(BF16)
            self.send(self.relayed.at[1], 4, 2)

        def total(self):
            total = self.value(z)
            for slot in (1, 2, 4, 3):
                total = total + self.wait(slot)
            return total

    z_conv = ZSum(
        0, lambda t: conv_send.at[t], lambda t: conv_sum[pl.ds(t, 1)][0], conv_got, conv_relay
    )
    z_parts = ZSum(
        1,
        lambda t: parts.at[:, t, pl.ds(80, 80)],
        lambda t: parts[:, pl.ds(t, 1), 80:160, :][:, 0].astype(F32),
        parts_got,
        parts_relay,
    )
    z_adapter = ZSum(
        2, lambda t: adapter_send.at[t], lambda t: adapter_sum[pl.ds(t, 1)][0], adapter_got, adapter_relay
    )

    for k, (owner, h, dev) in enumerate(
        ((xo, 0, to_right), (xo, 1, to_left), (xr, 1, to_right), (xl, 0, to_left))
    ):
        conv_part(owner, h)
        rs_send(halves(owner, h), k, dev)
    conv_part(xr, 0)
    conv_part(xl, 1)
    conv_part(x, 0)
    conv_part(x, 1)
    z_parts.first()

    for k, to in x_order:
        block = columns_in.at[k, half]
        arrived(block, x_ss.at[0, k], x_rs.at[0, k])
        go(block, block, x_ss.at[1, k], x_rs.at[1, k], mate)
    rs_second()

    routed(1)
    hidden_all[0] = unpack(slow, shigh, got[1]).astype(BF16)
    for k, to in x_order:
        go(hidden_all.at[0], hidden_all.at[k], x_ss.at[2, k], x_rs.at[2, k], at(to * NZ + z, f))
    adapter_quarter[...] = nn(hidden_all[0], prompt_ref[pl.ds(x, 1)][0])
    slope_ag.relay()
    slope_ag.near()
    for k, to in x_order:
        arrived(columns_in.at[k, other_half], x_ss.at[1, k], x_rs.at[1, k])
    rs_third()
    z_conv.first()
    z_parts.relay()

    for k, to in x_order[:2]:
        arrived(hidden_all.at[k], x_ss.at[2, k], x_rs.at[2, k])
        adapter_quarter[...] += nn(hidden_all[k], columns_in[k])
    k = x_order[2][0]
    arrived(hidden_all.at[k], x_ss.at[2, k], x_rs.at[2, k])
    quarter = adapter_quarter[...] + nn(hidden_all[k], columns_in[k])
    for q in range(NZ):
        chunk = quarter[:, ECOL * q : ECOL * q + ECOL]
        chunk = jnp.concatenate([chunk, jnp.zeros((CH, 128 - ECOL), F32)], axis=1)
        adapter_sum[q] = chunk
        adapter_send[q] = chunk.astype(BF16)
    z_adapter.first()
    z_conv.relay()
    lines = z_parts.total()
    parts_sum[...] = lines
    parts_send[...] = lines.astype(BF16)
    for k, to in x_order:
        go(parts_send.at[to], parts_last.at[k], x_ss.at[3, k], x_rs.at[3, k], at(to * NZ + z, f))

    def weight_come(k, carry):
        come = lax.rem(f + N_FSDP - k, N_FSDP)
        rcopy(
            weight_in.at[come], weight_in.at[come], w_ss.at[k], w_rs.at[k], at(d, come)
        ).wait_recv()
        return carry

    lax.fori_loop(1, N_FSDP, weight_come, 0)
    for g in range(N_FSDP):
        weight_own[:, CH * g : CH * g + CH] = weight_in[g].T
    z_adapter.relay()
    slope_ag.far()
    for k in range(4):
        slope_ag.from_mate(k)
    grads = nn(weight_own[...], slope_all[...].reshape(N_FSDP * CH, TOK))
    odd, even = [], []
    for q in range(4):
        lines = grads[128 * q : 128 * q + 128]
        odd.append(lines[:TAPC] + pltpu.roll(lines[2 * TAPC : 3 * TAPC] * inside, TOK - 1, 1))
        even.append(lines[TAPC : 2 * TAPC])
    odd = jnp.concatenate(odd, axis=0).astype(BF16)
    even = jnp.concatenate(even, axis=0).astype(BF16)
    for b in range(3):
        both = jnp.concatenate(
            [odd[:, 128 * b : 128 * b + 128], even[:, 128 * b : 128 * b + 128]], axis=1
        )
        hidden_ref[:, 256 * b : 256 * b + 256] = nt(both, halving[...]).astype(BF16)

    sums_ref[0, :80] = z_conv.total() * GRAD_SCALE
    total = parts_sum[pl.ds(x, 1)][0]
    for k, to in x_order:
        arrived(parts_last.at[k], x_ss.at[3, k], x_rs.at[3, k])
        total = total + parts_last[k].astype(F32)
    sums_ref[0, 80:] = total * GRAD_SCALE
    sums_ref[1] = z_adapter.total() * GRAD_SCALE

    for copy in pending:
        copy.wait_send()
    route_sent(0)
    route_sent(1)

    def weight_sent(k, carry):
        to = lax.rem(f + k, N_FSDP)
        rcopy(
            weight_t.at[:, pl.ds(pl.multiple_of(to * 512, 512), 512)], weight_in.at[f],
            w_ss.at[k], w_rs.at[k], at(d, to),
        ).wait_send()
        return carry

    lax.fori_loop(1, N_FSDP, weight_sent, 0)


def finish(hidden_in, sums_ref, hidden_ref, gadapter_ref, gconv_ref):
    hidden_ref[...] = hidden_in[...]
    conv = sums_ref[0].T
    gconv_ref[0] = conv[2 * TAPC : 3 * TAPC]
    gconv_ref[1] = conv[TAPC : 2 * TAPC]
    gconv_ref[2] = conv[:TAPC]
    gadapter_ref[...] = sums_ref[1][:, :ECOL]


def body(
    hidden_frames, conv_weight, conv_bias, adapter_weight, prompt_grad, token_index, clip_tokens
):
    vmem = pl.BlockSpec(memory_space=pltpu.VMEM)
    smem = pl.BlockSpec(memory_space=pltpu.SMEM)
    hbm = pl.BlockSpec(memory_space=pl.ANY)
    dma = pltpu.SemaphoreType.DMA
    hidden, sums = pl.pallas_call(
        kernel,
        out_shape=(
            jax.ShapeDtypeStruct((CH, 2 * TOK), BF16),
            jax.ShapeDtypeStruct((2, CH, 128), F32),
        ),
        in_specs=[hbm, hbm, vmem, hbm, hbm, vmem, smem],
        out_specs=(vmem, vmem),
        scratch_shapes=[
            pltpu.VMEM((N_FSDP, CH, 2 * TOK), BF16),
            pltpu.VMEM((3, CH, N_FSDP * CH), BF16),
            pltpu.VMEM((CH, WIDTH), BF16),
            pltpu.VMEM((NX, TOK, QUARTER), BF16),
            dma((7,)),
            pltpu.VMEM((256, 256), BF16),
            pltpu.VMEM((CH, TOK), F32),
            pltpu.VMEM((CH, TOK), F32),
            pltpu.VMEM((CH, N_DP * 128), BF16),
            pltpu.VMEM((N_FSDP, CH, 512), BF16),
            pltpu.VMEM((512, N_FSDP * CH), BF16),
            pltpu.VMEM((N_DP, 128, TOK), BF16),
            pltpu.VMEM((N_DP * CAP, TOK), BF16),
            pltpu.VMEM((4, N_DP * 8, TOK), BF16),
            pltpu.VMEM((N_DP * CAP, TOK), BF16),
            pltpu.VMEM((4, N_DP * 8, TOK), BF16),
            pltpu.VMEM((2, N_DP, 32, 128), BF16),
            pltpu.VMEM((2, N_DP, 32, 128), BF16),
            pltpu.VMEM((N_FSDP, CH, TOK), BF16),
            pltpu.VMEM((NX, TOK, QUARTER), BF16),
            pltpu.VMEM((NX, CH, TOK), BF16),
            pltpu.VMEM((CH, QUARTER), F32),
            pltpu.VMEM((NZ, CH, 128), F32),
            pltpu.VMEM((NX, NZ, CH, 128), BF16),
            pltpu.VMEM((6, 4, 80, 128), BF16),
            pltpu.VMEM((2, 4, 80, 128), BF16),
            pltpu.VMEM((NZ, 80, 128), F32),
            pltpu.VMEM((NZ, 80, 128), BF16),
            pltpu.VMEM((NZ, 80, 128), BF16),
            pltpu.VMEM((2, 80, 128), BF16),
            pltpu.VMEM((NZ, NX, 80, 128), BF16),
            pltpu.VMEM((2, NX, 80, 128), BF16),
            pltpu.VMEM((NX, 80, 128), F32),
            pltpu.VMEM((NX, 80, 128), BF16),
            pltpu.VMEM((NX, 80, 128), BF16),
            pltpu.VMEM((NZ, CH, 128), BF16),
            pltpu.VMEM((NZ, CH, 128), BF16),
            pltpu.VMEM((2, CH, 128), BF16),
            dma((2, N_DP)), dma((2, N_DP)),
            dma((2, 11)), dma((2, 11)),
            dma((N_FSDP,)), dma((N_FSDP,)),
            dma((6,)), dma((6,)),
            dma((3, NZ)), dma((3, NZ)),
            dma((4, NX)), dma((4, NX)),
        ],
        compiler_params=pltpu.CompilerParams(
            collective_id=0, has_side_effects=True, vmem_limit_bytes=56 * 1024 * 1024
        ),
    )(
        hidden_frames.T,
        jnp.swapaxes(conv_weight, 1, 2),
        conv_bias,
        adapter_weight,
        prompt_grad,
        token_index,
        clip_tokens,
    )
    hidden, gadapter, gconv = pl.pallas_call(
        finish,
        out_shape=(
            jax.ShapeDtypeStruct((CH, 2 * TOK), BF16),
            jax.ShapeDtypeStruct((CH, ECOL), F32),
            jax.ShapeDtypeStruct((3, TAPC, CH), F32),
        ),
        in_specs=[vmem, vmem],
        out_specs=(vmem, vmem, vmem),
    )(hidden, sums)
    return (hidden.T, gadapter, gconv)


def solution(mesh):
    placed = (
        P("dp", "fsdp"),
        P(None, None, "fsdp"),
        P("fsdp"),
        P("fsdp", None),
        P("dp", None),
        P("dp"),
        P("dp", None),
    )
    return jax.shard_map(
        body,
        mesh=mesh,
        in_specs=placed,
        out_specs=(P("dp", "fsdp"), P("fsdp", "dp"), P(None, "dp", "fsdp")),
        check_vma=False,
    )
```

```python
import math

import jax
import jax.numpy as jnp
from jax import lax
from jax.experimental import pallas as pl
from jax.experimental.pallas import tpu as pltpu
from jax.sharding import PartitionSpec as P

MESH = pl.DeviceIdType.MESH
F32 = jnp.float32
BF16 = jnp.bfloat16

NX, NZ, NY = 4, 8, 4
N_DP, N_FSDP = NX * NZ, 2 * NY
TOK = 384
CH = 160
WIDTH = 3584
CAP = 24
LOW = 128
ECOL = WIDTH // N_DP
XROWS = 48
ZROWS = CH - XROWS
QUARTER = WIDTH // NX
TAPC = 40
GRAD_SCALE = 1.0 / math.sqrt(TOK * N_DP)


def nn(left, right):
    return lax.dot_general(left, right, (((1,), (0,)), ((), ())), preferred_element_type=F32)


def nt(left, right):
    return lax.dot_general(left, right, (((1,), (1,)), ((), ())), preferred_element_type=F32)


def iota(shape, dim):
    return lax.broadcasted_iota(jnp.int32, shape, dim)


def pick(cond):
    return jnp.where(cond, 1.0, 0.0).astype(F32)


def low_hot(keys):
    rows = iota((N_DP, CAP, TOK), 1)
    return pick(keys[:, None, :] == rows).reshape(N_DP * CAP, TOK).astype(BF16)


def high_hot(keys, group):
    rows = iota((N_DP, 8, TOK), 1)
    hit = (keys[:, None, :] == rows + 6 * group) & (rows < 6)
    return pick(hit).reshape(N_DP * 8, TOK).astype(BF16)


def pack(low_ref, high_ref, rows_t, extra=None):
    low = nt(low_ref[...], rows_t[:LOW])
    tail = rows_t[LOW:]
    zero = jnp.zeros((CH - LOW, TOK), BF16)
    high = extra
    for group in range(4):
        placed = jnp.concatenate([tail if g == group else zero for g in range(4)], axis=0)
        part = nt(high_ref[group], placed)
        high = part if high is None else high + part
    slabs = jnp.concatenate([low.reshape(N_DP, CAP, 128), high.reshape(N_DP, 8, 128)], axis=1)
    return slabs.astype(BF16)


def unpack(low_ref, high_ref, got):
    got = got.astype(F32)
    low = got[:, :CAP, :].reshape(N_DP * CAP, 128).T.astype(BF16)
    high = got[:, CAP:, :].reshape(N_DP * 8, 128).T.astype(BF16)
    low = nn(low, low_ref[...])
    tail = None
    for group in range(4):
        part = nn(high[32 * group : 32 * group + 32], high_ref[group])
        tail = part if tail is None else tail + part
    return jnp.concatenate([low, tail], axis=0)


def kernel(
    frames_hbm, weight_hbm, bias_ref, adapter_hbm, prompt_hbm, index_ref, clips_ref,
    hidden_ref, sums_ref,
    frames_all, weight_ref, adapter_ref, prompt_ref, in_sem, halving,
    preact_ref, back_ref, weight_t, weight_in, weight_own, xbuf,
    slow, shigh, dlow, dhigh, send, got, slope_all,
    columns_in, hidden_all, adapter_quarter, adapter_sum,
    parts, rs_in, rs_out, conv_sum, conv_send, conv_got, conv_relay,
    parts_got, parts_relay, parts_sum, parts_send, parts_last,
    adapter_send, adapter_got, adapter_relay,
    route_ss, route_rs, ag_ss, ag_rs, w_ss, w_rs, rs_ss, rs_rs, z_ss, z_rs, x_ss, x_rs,
):
    d = lax.axis_index("dp")
    f = lax.axis_index("fsdp")
    x, z = d // NZ, lax.rem(d, NZ)
    y, c = f // 2, lax.rem(f, 2)
    pending = []
    loads = [
        pltpu.make_async_copy(src, dst, in_sem.at[k])
        for k, (src, dst) in enumerate(
            (
                (frames_hbm, frames_all.at[f]),
                *(
                    (prompt_hbm.at[:, pl.ds(QUARTER * q, QUARTER)], prompt_ref.at[q])
                    for q in range(NX)
                ),
                (adapter_hbm, adapter_ref),
                (weight_hbm, weight_ref),
            )
        )
    ]
    for load in loads:
        load.start()

    def at(dp, fs):
        return {"dp": dp, "fsdp": fs}

    def rcopy(src, dst, ssem, rsem, dev):
        return pltpu.make_async_remote_copy(
            src_ref=src, dst_ref=dst, send_sem=ssem, recv_sem=rsem,
            device_id=dev, device_id_type=MESH,
        )

    def go(src, dst, ssem, rsem, dev):
        copy = rcopy(src, dst, ssem, rsem, dev)
        copy.start()
        pending.append(copy)

    def arrived(dst, ssem, rsem):
        rcopy(dst, dst, ssem, rsem, at(d, f)).wait_recv()

    barrier = pltpu.get_barrier_semaphore()

    def greet_dp(k, carry):
        pl.semaphore_signal(
            barrier, inc=1, device_id=at(lax.rem(d + k, N_DP), f), device_id_type=MESH
        )
        return carry

    def greet_fsdp(k, carry):
        pl.semaphore_signal(
            barrier, inc=1, device_id=at(d, lax.rem(f + k, N_FSDP)), device_id_type=MESH
        )
        return carry

    lax.fori_loop(1, N_DP, greet_dp, 0)
    lax.fori_loop(1, N_FSDP, greet_fsdp, 0)

    pl.semaphore_wait(barrier, N_DP - 1 + N_FSDP - 1)

    yr, yl, yo = lax.rem(y + 1, NY), lax.rem(y + NY - 1, NY), lax.rem(y + 2, NY)
    mate = at(d, y * 2 + 1 - c)

    class Gather:
        def __init__(self, which, own, buf):
            self.ss, self.rs = ag_ss.at[which], ag_rs.at[which]
            self.own, self.buf = own, buf

        def send(self, src, dst, k, dev):
            go(src, dst, self.ss.at[k], self.rs.at[k], dev)

        def half(self, g, h):
            return self.buf.at[g, pl.ds(80 * h, 80)]

        def come(self, dst, k):
            arrived(dst, self.ss.at[k], self.rs.at[k])

        def first(self):
            for h in range(2):
                for k, (to, part) in enumerate(((yr, h), (yl, 1 - h))):
                    src = self.own.at[pl.ds(80 * part, 80)]
                    self.send(src, self.half(f, part), 2 * k + part, at(d, to * 2 + c))
            self.send(self.own, self.buf.at[f], 6, mate)

        def relay(self):
            for k, (come, to) in enumerate(((yl, yr), (yr, yl))):
                block = self.half(come * 2 + c, k)
                self.come(block, 2 * k + k)
                self.send(block, block, 4 + k, at(d, to * 2 + c))

        def near(self):
            for k, come in enumerate((yl, yr)):
                self.come(self.half(come * 2 + c, 1 - k), 2 * k + 1 - k)
                block = self.buf.at[come * 2 + c]
                self.send(block, block, 7 + k, mate)

        def far(self):
            for h in range(2):
                block = self.half(yo * 2 + c, h)
                self.come(block, 4 + h)
                self.send(block, block, 9 + h, mate)

        def from_mate(self, k):
            o = 1 - c
            if k < 3:
                self.come(self.buf.at[(y, yl, yr)[k] * 2 + o], 6 + k)
            else:
                self.come(self.half(yo * 2 + o, 0), 9)
                self.come(self.half(yo * 2 + o, 1), 10)

    frames_ag = Gather(0, frames_hbm, frames_all)
    frames_ag.first()

    row = iota((256, 256), 0)
    col = iota((256, 256), 1)
    halving[...] = pick(row == jnp.where(col < 128, 2 * col + 1, 2 * (col - 128))).astype(BF16)

    index = index_ref[...].reshape(1, TOK)
    group = iota((N_DP, TOK), 0)
    mine = (index >= group * TOK) & (index < (group + 1) * TOK)
    member = pick(mine)
    before = pick(iota((TOK, TOK), 0) < iota((TOK, TOK), 1)).astype(BF16)
    rank = nn(member.astype(BF16), before)
    local = index - jnp.sum(jnp.where(mine, group, 0), axis=0, keepdims=True) * TOK
    keys = jnp.where(mine, rank.astype(jnp.int32), -1)
    slow[...] = low_hot(keys)
    for g in range(4):
        shigh[g] = high_hot(keys, g)
    own_rank = jnp.max(keys, axis=0, keepdims=True)
    by_rank = pick(iota((128, TOK), 0) == own_rank).astype(BF16)
    part = iota((N_DP, 8, TOK), 1)
    high_bits = jnp.where(mine, (local >> 4) + 1, 0).astype(F32)
    low_bits = jnp.where(mine, local & 15, 0).astype(F32)
    marks = jnp.where(part == 6, high_bits[:, None, :], jnp.where(part == 7, low_bits[:, None, :], 0.0))
    extra = nt(marks.reshape(N_DP * 8, TOK).astype(BF16), by_rank)

    for q in range(NX):
        loads[1 + q].wait()
    loads[5].wait()
    back_t = nt(adapter_ref[:, :QUARTER], prompt_ref[0])
    for q in range(1, NX):
        back_t = back_t + nt(adapter_ref[:, QUARTER * q : QUARTER * q + QUARTER], prompt_ref[q])
    back_t = back_t.astype(BF16)
    send[0] = pack(slow, shigh, back_t, extra)

    def route(which):
        def step(k, carry):
            to = lax.rem(d + k, N_DP)
            rcopy(
                send.at[which, to], got.at[which, d],
                route_ss.at[which, k], route_rs.at[which, k], at(to, f),
            ).start()
            return carry

        lax.fori_loop(1, N_DP, step, 0)
        got[which, pl.ds(d, 1)] = send[which, pl.ds(d, 1)]

    def routed(which):
        def step(k, carry):
            come = lax.rem(d + N_DP - k, N_DP)
            rcopy(
                got.at[which, come], got.at[which, come],
                route_ss.at[which, k], route_rs.at[which, k], at(come, f),
            ).wait_recv()
            return carry

        lax.fori_loop(1, N_DP, step, 0)

    def route_sent(which):
        def step(k, carry):
            to = lax.rem(d + k, N_DP)
            rcopy(
                send.at[which, to], got.at[which, d],
                route_ss.at[which, k], route_rs.at[which, k], at(to, f),
            ).wait_send()
            return carry

        lax.fori_loop(1, N_DP, step, 0)

    route(0)

    xr, xl, xo = lax.rem(x + 1, NX), lax.rem(x + NX - 1, NX), lax.rem(x + 2, NX)
    x_order = ((1, xr), (3, xl), (2, xo))
    half = pl.ds(pl.multiple_of(192 * c, 192), 192)
    other_half = pl.ds(pl.multiple_of(192 - 192 * c, 192), 192)
    for k, to in x_order:
        go(
            prompt_ref.at[to, half],
            columns_in.at[k, half],
            x_ss.at[0, k], x_rs.at[0, k], at(to * NZ + z, f),
        )

    loads[6].wait()
    pad8 = jnp.zeros((CH, 8), BF16)
    for o in range(N_DP):
        lines = [weight_ref[k, :, TAPC * o : TAPC * o + TAPC] for k in (2, 1, 0)]
        weight_t[:, 128 * o : 128 * o + 128] = jnp.concatenate(lines + [pad8], axis=1)

    lane = iota((1, TOK), 1)
    inside = jnp.ones((1, TOK), F32)
    start = jnp.int32(0)
    for k in range(6):
        inside = jnp.where(lane == start, 0.0, inside)
        start = start + clips_ref[0, k]
    pad_rows = jnp.zeros((8, TOK), F32)

    bias = bias_ref[...].astype(F32).reshape(1, CH)
    bias = jnp.sum(jnp.where(iota((CH, CH), 0) == iota((CH, CH), 1), bias, 0.0), axis=1, keepdims=True)
    preact_ref[...] = jnp.broadcast_to(bias, (CH, TOK))

    def preact_block(g):
        lines = [
            nn(frames_all[pl.ds(g, 1), :, 256 * b : 256 * b + 256][0], halving[...]) for b in range(3)
        ]
        odd = jnp.concatenate([part[:, :128] for part in lines], axis=1)
        even = jnp.concatenate([part[:, 128:] for part in lines], axis=1)
        early = pltpu.roll(odd, 1, 1) * inside
        blocks = []
        for q in range(4):
            rows = slice(TAPC * q, TAPC * q + TAPC)
            blocks += [odd[rows], even[rows], early[rows], pad_rows]
        block = jnp.concatenate(blocks, axis=0).astype(BF16)
        xbuf[pl.ds(4 * g, 4)] = block.reshape(4, 128, TOK)
        preact_ref[...] += nn(weight_t[:, pl.ds(pl.multiple_of(g * 512, 512), 512)], block)

    loads[0].wait()
    preact_block(f)
    frames_ag.relay()
    frames_ag.from_mate(0)
    preact_block(y * 2 + 1 - c)
    frames_ag.near()
    preact_block(yl * 2 + c)
    preact_block(yr * 2 + c)
    frames_ag.far()

    def weight_out(k, carry):
        to = lax.rem(f + k, N_FSDP)
        rcopy(
            weight_t.at[:, pl.ds(pl.multiple_of(to * 512, 512), 512)], weight_in.at[f],
            w_ss.at[k], w_rs.at[k], at(d, to),
        ).start()
        return carry

    lax.fori_loop(1, N_FSDP, weight_out, 0)
    weight_in[pl.ds(f, 1)] = weight_t[:, pl.ds(pl.multiple_of(f * 512, 512), 512)][None]

    preact_block(yo * 2 + c)

    routed(0)
    tags = got[0, :, CAP:, :].astype(F32)
    numbers = (tags[:, 6, :] - 1.0) * 16.0 + tags[:, 7, :]

    def token_of(rows, first, most):
        spot = iota((N_DP, rows, 128), 1)
        match = (iota((N_DP, rows, 128), 2) == spot + first) & (spot < most)
        picked = jnp.sum(jnp.where(match, numbers[:, None, :], 0.0), axis=2, keepdims=True)
        ok = iota((N_DP, rows, 1), 1) < most
        return jnp.where(ok, picked, -1.0)

    def token_hot(rows, first, most):
        token = iota((N_DP, rows, TOK), 2).astype(F32)
        return pick(token_of(rows, first, most) == token).reshape(N_DP * rows, TOK).astype(BF16)

    dlow[...] = token_hot(CAP, 0, CAP)
    for g in range(4):
        dhigh[g] = token_hot(8, 6 * g, 6)
    back_ref[...] = unpack(dlow, dhigh, got[0])

    for k, come in ((1, yl), (2, yr), (3, yo)):
        frames_ag.from_mate(k)
        preact_block(come * 2 + 1 - c)

    preact = preact_ref[...]
    cumul = 0.5 * (1.0 + lax.erf(preact * (1.0 / math.sqrt(2.0))))
    hidden_t = (preact * cumul).astype(BF16)
    send[1] = pack(dlow, dhigh, hidden_t)
    route(1)

    slope = cumul + preact * jnp.exp(-0.5 * preact * preact) * (1.0 / math.sqrt(2.0 * math.pi))
    slope_t = (back_ref[...] * slope).astype(BF16)
    slope_all[pl.ds(f, 1)] = slope_t[None]
    slope_ag = Gather(1, slope_all.at[f], slope_all)
    slope_ag.first()

    to_right, to_left = at(xr * NZ + z, f), at(xl * NZ + z, f)

    def halves(owner, h):
        return parts.at[owner, pl.ds(4 * h, 4), pl.ds(0, XROWS)]

    def rs_send(src, k, dev):
        go(src, rs_in.at[k], rs_ss.at[k], rs_rs.at[k], dev)

    def rs_wait(k):
        arrived(rs_in.at[k], rs_ss.at[k], rs_rs.at[k])

    def conv_part(owner, h):
        g = 2 * owner + h
        block = nt(slope_t, xbuf[pl.ds(4 * g, 4)].reshape(512, TOK))
        for q in range(4):
            parts[pl.ds(owner, 1), 4 * h + q] = block[:, 128 * q : 128 * q + 128].astype(BF16)[None]

    def rs_second():
        for k, owner, dev in ((0, xr, to_right), (1, xl, to_left)):
            rs_wait(k)
            total = halves(owner, k)[...].astype(F32) + rs_in[k].astype(F32)
            rs_out[k] = total.astype(BF16)
            rs_send(rs_out.at[k], 4 + k, dev)

    def rs_third():
        for k in (2, 3, 4, 5):
            rs_wait(k)
        for h, (one, two) in enumerate(((4, 3), (5, 2))):
            total = halves(x, h)[...].astype(F32) + rs_in[one].astype(F32)
            total = total + rs_in[two].astype(F32)
            conv_sum[pl.ds(4 * h, 4)] = total
            conv_send[pl.ds(4 * h, 4)] = total.astype(BF16)

    def z_at(offset):
        return lax.rem(z + NZ + offset, NZ)

    class ZSum:
        def __init__(self, which, chunk, value, dst, relay):
            self.ss, self.rs = z_ss.at[which], z_rs.at[which]
            self.chunk, self.value, self.dst, self.relayed = chunk, value, dst, relay

        def send(self, src, slot, to):
            go(src, self.dst.at[slot], self.ss.at[slot], self.rs.at[slot], at(x * NZ + z_at(to), f))

        def wait(self, slot):
            arrived(self.dst.at[slot], self.ss.at[slot], self.rs.at[slot])
            return self.dst[slot].astype(F32)

        def first(self):
            for slot, chunk, to in ((5, -4, -2), (6, -3, -1), (7, 3, 1), (1, 1, 1), (2, -1, -1)):
                self.send(self.chunk(z_at(chunk)), slot, to)

        def relay(self):
            total = self.value(z_at(-2)) + self.wait(5) + self.wait(6)
            self.relayed[0] = total.astype(BF16)
            self.send(self.relayed.at[0], 3, -2)
            self.relayed[1] = (self.value(z_at(2)) + self.wait(7)).astype(BF16)
            self.send(self.relayed.at[1], 4, 2)

        def total(self):
            total = self.value(z)
            for slot in (1, 2, 4, 3):
                total = total + self.wait(slot)
            return total

    z_conv = ZSum(
        0, lambda t: conv_send.at[t], lambda t: conv_sum[pl.ds(t, 1)][0], conv_got, conv_relay
    )
    z_parts = ZSum(
        1,
        lambda t: parts.at[:, t, pl.ds(XROWS, ZROWS)],
        lambda t: parts[:, pl.ds(t, 1), XROWS:, :][:, 0].astype(F32),
        parts_got,
        parts_relay,
    )
    z_adapter = ZSum(
        2, lambda t: adapter_send.at[t], lambda t: adapter_sum[pl.ds(t, 1)][0], adapter_got, adapter_relay
    )

    for k, (owner, h, dev) in enumerate(
        ((xo, 0, to_right), (xo, 1, to_left), (xr, 1, to_right), (xl, 0, to_left))
    ):
        conv_part(owner, h)
        rs_send(halves(owner, h), k, dev)
    conv_part(xr, 0)
    conv_part(xl, 1)
    conv_part(x, 0)
    conv_part(x, 1)
    z_parts.first()

    for k, to in x_order:
        block = columns_in.at[k, half]
        arrived(block, x_ss.at[0, k], x_rs.at[0, k])
        go(block, block, x_ss.at[1, k], x_rs.at[1, k], mate)

    rs_second()

    routed(1)
    hidden_all[0] = unpack(slow, shigh, got[1]).astype(BF16)
    for k, to in x_order:
        go(hidden_all.at[0], hidden_all.at[k], x_ss.at[2, k], x_rs.at[2, k], at(to * NZ + z, f))
    adapter_quarter[...] = nn(hidden_all[0], prompt_ref[pl.ds(x, 1)][0])
    slope_ag.relay()
    slope_ag.near()
    for k, to in x_order:
        arrived(columns_in.at[k, other_half], x_ss.at[1, k], x_rs.at[1, k])
    rs_third()
    z_conv.first()
    z_parts.relay()

    for k, to in x_order[:2]:
        arrived(hidden_all.at[k], x_ss.at[2, k], x_rs.at[2, k])
        adapter_quarter[...] += nn(hidden_all[k], columns_in[k])
    k = x_order[2][0]
    arrived(hidden_all.at[k], x_ss.at[2, k], x_rs.at[2, k])
    quarter = adapter_quarter[...] + nn(hidden_all[k], columns_in[k])
    for q in range(NZ):
        chunk = quarter[:, ECOL * q : ECOL * q + ECOL]
        chunk = jnp.concatenate([chunk, jnp.zeros((CH, 128 - ECOL), F32)], axis=1)
        adapter_sum[q] = chunk
        adapter_send[q] = chunk.astype(BF16)
    z_adapter.first()
    z_conv.relay()
    lines = z_parts.total()
    parts_sum[...] = lines
    parts_send[...] = lines.astype(BF16)
    for k, to in x_order:
        go(parts_send.at[to], parts_last.at[k], x_ss.at[3, k], x_rs.at[3, k], at(to * NZ + z, f))

    def weight_come(k, carry):
        come = lax.rem(f + N_FSDP - k, N_FSDP)
        rcopy(
            weight_in.at[come], weight_in.at[come], w_ss.at[k], w_rs.at[k], at(d, come)
        ).wait_recv()
        return carry

    lax.fori_loop(1, N_FSDP, weight_come, 0)
    for g in range(N_FSDP):
        weight_own[:, CH * g : CH * g + CH] = weight_in[g].T
    z_adapter.relay()
    slope_ag.far()
    for k in range(4):
        slope_ag.from_mate(k)
    grads = nn(weight_own[...], slope_all[...].reshape(N_FSDP * CH, TOK))
    odd, even = [], []
    for q in range(4):
        lines = grads[128 * q : 128 * q + 128]
        odd.append(lines[:TAPC] + pltpu.roll(lines[2 * TAPC : 3 * TAPC] * inside, TOK - 1, 1))
        even.append(lines[TAPC : 2 * TAPC])
    odd = jnp.concatenate(odd, axis=0).astype(BF16)
    even = jnp.concatenate(even, axis=0).astype(BF16)
    for b in range(3):
        both = jnp.concatenate(
            [odd[:, 128 * b : 128 * b + 128], even[:, 128 * b : 128 * b + 128]], axis=1
        )
        hidden_ref[:, 256 * b : 256 * b + 256] = nt(both, halving[...]).astype(BF16)

    sums_ref[0, :XROWS] = z_conv.total() * GRAD_SCALE
    total = parts_sum[pl.ds(x, 1)][0]
    for k, to in x_order:
        arrived(parts_last.at[k], x_ss.at[3, k], x_rs.at[3, k])
        total = total + parts_last[k].astype(F32)
    sums_ref[0, XROWS:] = total * GRAD_SCALE
    sums_ref[1] = z_adapter.total() * GRAD_SCALE

    for copy in pending:
        copy.wait_send()
    route_sent(0)
    route_sent(1)

    def weight_sent(k, carry):
        to = lax.rem(f + k, N_FSDP)
        rcopy(
            weight_t.at[:, pl.ds(pl.multiple_of(to * 512, 512), 512)], weight_in.at[f],
            w_ss.at[k], w_rs.at[k], at(d, to),
        ).wait_send()
        return carry

    lax.fori_loop(1, N_FSDP, weight_sent, 0)


def finish(hidden_in, sums_ref, hidden_ref, gadapter_ref, gconv_ref):
    hidden_ref[...] = hidden_in[...]
    conv = sums_ref[0].T
    gconv_ref[0] = conv[2 * TAPC : 3 * TAPC]
    gconv_ref[1] = conv[TAPC : 2 * TAPC]
    gconv_ref[2] = conv[:TAPC]
    gadapter_ref[...] = sums_ref[1][:, :ECOL]


def body(
    hidden_frames, conv_weight, conv_bias, adapter_weight, prompt_grad, token_index, clip_tokens
):
    vmem = pl.BlockSpec(memory_space=pltpu.VMEM)
    smem = pl.BlockSpec(memory_space=pltpu.SMEM)
    hbm = pl.BlockSpec(memory_space=pl.ANY)
    dma = pltpu.SemaphoreType.DMA
    hidden, sums = pl.pallas_call(
        kernel,
        out_shape=(
            jax.ShapeDtypeStruct((CH, 2 * TOK), BF16),
            jax.ShapeDtypeStruct((2, CH, 128), F32),
        ),
        in_specs=[hbm, hbm, vmem, hbm, hbm, vmem, smem],
        out_specs=(vmem, vmem),
        scratch_shapes=[
            pltpu.VMEM((N_FSDP, CH, 2 * TOK), BF16),
            pltpu.VMEM((3, CH, N_FSDP * CH), BF16),
            pltpu.VMEM((CH, WIDTH), BF16),
            pltpu.VMEM((NX, TOK, QUARTER), BF16),
            dma((7,)),
            pltpu.VMEM((256, 256), BF16),
            pltpu.VMEM((CH, TOK), F32),
            pltpu.VMEM((CH, TOK), F32),
            pltpu.VMEM((CH, N_DP * 128), BF16),
            pltpu.VMEM((N_FSDP, CH, 512), BF16),
            pltpu.VMEM((512, N_FSDP * CH), BF16),
            pltpu.VMEM((N_DP, 128, TOK), BF16),
            pltpu.VMEM((N_DP * CAP, TOK), BF16),
            pltpu.VMEM((4, N_DP * 8, TOK), BF16),
            pltpu.VMEM((N_DP * CAP, TOK), BF16),
            pltpu.VMEM((4, N_DP * 8, TOK), BF16),
            pltpu.VMEM((2, N_DP, 32, 128), BF16),
            pltpu.VMEM((2, N_DP, 32, 128), BF16),
            pltpu.VMEM((N_FSDP, CH, TOK), BF16),
            pltpu.VMEM((NX, TOK, QUARTER), BF16),
            pltpu.VMEM((NX, CH, TOK), BF16),
            pltpu.VMEM((CH, QUARTER), F32),
            pltpu.VMEM((NZ, CH, 128), F32),
            pltpu.VMEM((NX, NZ, CH, 128), BF16),
            pltpu.VMEM((6, 4, XROWS, 128), BF16),
            pltpu.VMEM((2, 4, XROWS, 128), BF16),
            pltpu.VMEM((NZ, XROWS, 128), F32),
            pltpu.VMEM((NZ, XROWS, 128), BF16),
            pltpu.VMEM((NZ, XROWS, 128), BF16),
            pltpu.VMEM((2, XROWS, 128), BF16),
            pltpu.VMEM((NZ, NX, ZROWS, 128), BF16),
            pltpu.VMEM((2, NX, ZROWS, 128), BF16),
            pltpu.VMEM((NX, ZROWS, 128), F32),
            pltpu.VMEM((NX, ZROWS, 128), BF16),
            pltpu.VMEM((NX, ZROWS, 128), BF16),
            pltpu.VMEM((NZ, CH, 128), BF16),
            pltpu.VMEM((NZ, CH, 128), BF16),
            pltpu.VMEM((2, CH, 128), BF16),
            dma((2, N_DP)), dma((2, N_DP)),
            dma((2, 11)), dma((2, 11)),
            dma((N_FSDP,)), dma((N_FSDP,)),
            dma((6,)), dma((6,)),
            dma((3, NZ)), dma((3, NZ)),
            dma((4, NX)), dma((4, NX)),
        ],
        compiler_params=pltpu.CompilerParams(
            collective_id=0, has_side_effects=True, vmem_limit_bytes=56 * 1024 * 1024
        ),
    )(
        hidden_frames.T,
        jnp.swapaxes(conv_weight, 1, 2),
        conv_bias,
        adapter_weight,
        prompt_grad,
        token_index,
        clip_tokens,
    )
    hidden, gadapter, gconv = pl.pallas_call(
        finish,
        out_shape=(
            jax.ShapeDtypeStruct((CH, 2 * TOK), BF16),
            jax.ShapeDtypeStruct((CH, ECOL), F32),
            jax.ShapeDtypeStruct((3, TAPC, CH), F32),
        ),
        in_specs=[vmem, vmem],
        out_specs=(vmem, vmem, vmem),
    )(hidden, sums)
    return (hidden.T, gadapter, gconv)


def solution(mesh):
    placed = (
        P("dp", "fsdp"),
        P(None, None, "fsdp"),
        P("fsdp"),
        P("fsdp", None),
        P("dp", None),
        P("dp"),
        P("dp", None),
    )
    return jax.shard_map(
        body,
        mesh=mesh,
        in_specs=placed,
        out_specs=(P("dp", "fsdp"), P("fsdp", "dp"), P(None, "dp", "fsdp")),
        check_vma=False,
    )
```

```python
import math

import jax
import jax.numpy as jnp
from jax import lax
from jax.experimental import pallas as pl
from jax.experimental.pallas import tpu as pltpu
from jax.sharding import PartitionSpec as P

MESH = pl.DeviceIdType.MESH
F32 = jnp.float32
BF16 = jnp.bfloat16

NX, NZ, NY = 4, 8, 4
N_DP, N_FSDP = NX * NZ, 2 * NY
TOK = 384
CH = 160
WIDTH = 3584
CAP = 24
LOW = 128
ECOL = WIDTH // N_DP
XROWS = 48
ZROWS = CH - XROWS
QUARTER = WIDTH // NX
TAPC = 40
GRAD_SCALE = 1.0 / math.sqrt(TOK * N_DP)


def nn(left, right):
    return lax.dot_general(left, right, (((1,), (0,)), ((), ())), preferred_element_type=F32)


def nt(left, right):
    return lax.dot_general(left, right, (((1,), (1,)), ((), ())), preferred_element_type=F32)


def iota(shape, dim):
    return lax.broadcasted_iota(jnp.int32, shape, dim)


def pick(cond):
    return jnp.where(cond, 1.0, 0.0).astype(F32)


def low_hot(keys):
    rows = iota((N_DP, CAP, TOK), 1)
    return pick(keys[:, None, :] == rows).reshape(N_DP * CAP, TOK).astype(BF16)


def high_hot(keys, group):
    rows = iota((N_DP, 8, TOK), 1)
    hit = (keys[:, None, :] == rows + 6 * group) & (rows < 6)
    return pick(hit).reshape(N_DP * 8, TOK).astype(BF16)


def pack(low_ref, high_ref, rows_t, extra=None):
    low = nt(low_ref[...], rows_t[:LOW])
    tail = rows_t[LOW:]
    zero = jnp.zeros((CH - LOW, TOK), BF16)
    high = extra
    for group in range(4):
        placed = jnp.concatenate([tail if g == group else zero for g in range(4)], axis=0)
        part = nt(high_ref[group], placed)
        high = part if high is None else high + part
    slabs = jnp.concatenate([low.reshape(N_DP, CAP, 128), high.reshape(N_DP, 8, 128)], axis=1)
    return slabs.astype(BF16)


def unpack(low_ref, high_ref, got):
    got = got.astype(F32)
    low = got[:, :CAP, :].reshape(N_DP * CAP, 128).T.astype(BF16)
    high = got[:, CAP:, :].reshape(N_DP * 8, 128).T.astype(BF16)
    low = nn(low, low_ref[...])
    tail = None
    for group in range(4):
        part = nn(high[32 * group : 32 * group + 32], high_ref[group])
        tail = part if tail is None else tail + part
    return jnp.concatenate([low, tail], axis=0)


def kernel(
    frames_hbm, weight_hbm, bias_ref, adapter_hbm, prompt_hbm, index_ref, clips_ref,
    hidden_ref, sums_ref,
    frames_all, weight_ref, adapter_ref, prompt_ref, in_sem, halving,
    preact_ref, back_ref, weight_t, weight_in, weight_own, xbuf,
    slow, shigh, dlow, dhigh, send, got, slope_all,
    columns_in, hidden_all, adapter_quarter, adapter_sum,
    parts, rs_in, rs_out, conv_sum, conv_send, conv_got, conv_relay,
    parts_got, parts_relay, parts_sum, parts_send, parts_last,
    adapter_send, adapter_got, adapter_relay,
    route_ss, route_rs, ag_ss, ag_rs, w_ss, w_rs, rs_ss, rs_rs, z_ss, z_rs, x_ss, x_rs,
):
    d = lax.axis_index("dp")
    f = lax.axis_index("fsdp")
    x, z = d // NZ, lax.rem(d, NZ)
    y, c = f // 2, lax.rem(f, 2)
    pending = []
    loads = [
        pltpu.make_async_copy(src, dst, in_sem.at[k])
        for k, (src, dst) in enumerate(
            (
                (frames_hbm, frames_all.at[f]),
                *(
                    (prompt_hbm.at[:, pl.ds(QUARTER * q, QUARTER)], prompt_ref.at[q])
                    for q in range(NX)
                ),
                (adapter_hbm, adapter_ref),
                (weight_hbm, weight_ref),
            )
        )
    ]
    for load in loads:
        load.start()

    def at(dp, fs):
        return {"dp": dp, "fsdp": fs}

    def rcopy(src, dst, ssem, rsem, dev):
        return pltpu.make_async_remote_copy(
            src_ref=src, dst_ref=dst, send_sem=ssem, recv_sem=rsem,
            device_id=dev, device_id_type=MESH,
        )

    def go(src, dst, ssem, rsem, dev):
        copy = rcopy(src, dst, ssem, rsem, dev)
        copy.start()
        pending.append(copy)

    def arrived(dst, ssem, rsem):
        rcopy(dst, dst, ssem, rsem, at(d, f)).wait_recv()

    barrier = pltpu.get_barrier_semaphore()

    def greet_dp(k, carry):
        pl.semaphore_signal(
            barrier, inc=1, device_id=at(lax.rem(d + k, N_DP), f), device_id_type=MESH
        )
        return carry

    def greet_fsdp(k, carry):
        pl.semaphore_signal(
            barrier, inc=1, device_id=at(d, lax.rem(f + k, N_FSDP)), device_id_type=MESH
        )
        return carry

    lax.fori_loop(1, N_DP, greet_dp, 0)
    lax.fori_loop(1, N_FSDP, greet_fsdp, 0)

    pl.semaphore_wait(barrier, N_DP - 1 + N_FSDP - 1)

    yr, yl, yo = lax.rem(y + 1, NY), lax.rem(y + NY - 1, NY), lax.rem(y + 2, NY)
    mate = at(d, y * 2 + 1 - c)

    class Gather:
        def __init__(self, which, own, buf):
            self.ss, self.rs = ag_ss.at[which], ag_rs.at[which]
            self.own, self.buf = own, buf

        def send(self, src, dst, k, dev):
            go(src, dst, self.ss.at[k], self.rs.at[k], dev)

        def half(self, g, h):
            return self.buf.at[g, pl.ds(80 * h, 80)]

        def come(self, dst, k):
            arrived(dst, self.ss.at[k], self.rs.at[k])

        def first(self):
            for h in range(2):
                for k, (to, part) in enumerate(((yr, h), (yl, 1 - h))):
                    src = self.own.at[pl.ds(80 * part, 80)]
                    self.send(src, self.half(f, part), 2 * k + part, at(d, to * 2 + c))
            self.send(self.own, self.buf.at[f], 6, mate)

        def relay(self):
            for k, (come, to) in enumerate(((yl, yr), (yr, yl))):
                block = self.half(come * 2 + c, k)
                self.come(block, 2 * k + k)
                self.send(block, block, 4 + k, at(d, to * 2 + c))

        def near(self):
            for k, come in enumerate((yl, yr)):
                self.come(self.half(come * 2 + c, 1 - k), 2 * k + 1 - k)
                block = self.buf.at[come * 2 + c]
                self.send(block, block, 7 + k, mate)

        def far(self):
            for h in range(2):
                block = self.half(yo * 2 + c, h)
                self.come(block, 4 + h)
                self.send(block, block, 9 + h, mate)

        def from_mate(self, k):
            o = 1 - c
            if k < 3:
                self.come(self.buf.at[(y, yl, yr)[k] * 2 + o], 6 + k)
            else:
                self.come(self.half(yo * 2 + o, 0), 9)
                self.come(self.half(yo * 2 + o, 1), 10)

    frames_ag = Gather(0, frames_hbm, frames_all)
    frames_ag.first()

    row = iota((256, 256), 0)
    col = iota((256, 256), 1)
    halving[...] = pick(row == jnp.where(col < 128, 2 * col + 1, 2 * (col - 128))).astype(BF16)

    index = index_ref[...].reshape(1, TOK)
    group = iota((N_DP, TOK), 0)
    mine = (index >= group * TOK) & (index < (group + 1) * TOK)
    member = pick(mine)
    before = pick(iota((TOK, TOK), 0) < iota((TOK, TOK), 1)).astype(BF16)
    rank = nn(member.astype(BF16), before)
    local = index - jnp.sum(jnp.where(mine, group, 0), axis=0, keepdims=True) * TOK
    keys = jnp.where(mine, rank.astype(jnp.int32), -1)
    slow[...] = low_hot(keys)
    for g in range(4):
        shigh[g] = high_hot(keys, g)
    own_rank = jnp.max(keys, axis=0, keepdims=True)
    by_rank = pick(iota((128, TOK), 0) == own_rank).astype(BF16)
    part = iota((N_DP, 8, TOK), 1)
    high_bits = jnp.where(mine, (local >> 4) + 1, 0).astype(F32)
    low_bits = jnp.where(mine, local & 15, 0).astype(F32)
    marks = jnp.where(part == 6, high_bits[:, None, :], jnp.where(part == 7, low_bits[:, None, :], 0.0))
    extra = nt(marks.reshape(N_DP * 8, TOK).astype(BF16), by_rank)

    for q in range(NX):
        loads[1 + q].wait()
    loads[5].wait()
    back_t = nt(adapter_ref[:, :QUARTER], prompt_ref[0])
    for q in range(1, NX):
        back_t = back_t + nt(adapter_ref[:, QUARTER * q : QUARTER * q + QUARTER], prompt_ref[q])
    back_t = back_t.astype(BF16)
    send[0] = pack(slow, shigh, back_t, extra)

    def route(which):
        def step(k, carry):
            to = lax.rem(d + k, N_DP)
            rcopy(
                send.at[which, to], got.at[which, d],
                route_ss.at[which, k], route_rs.at[which, k], at(to, f),
            ).start()
            return carry

        lax.fori_loop(1, N_DP, step, 0)
        got[which, pl.ds(d, 1)] = send[which, pl.ds(d, 1)]

    def routed(which):
        def step(k, carry):
            come = lax.rem(d + N_DP - k, N_DP)
            rcopy(
                got.at[which, come], got.at[which, come],
                route_ss.at[which, k], route_rs.at[which, k], at(come, f),
            ).wait_recv()
            return carry

        lax.fori_loop(1, N_DP, step, 0)

    def route_sent(which):
        def step(k, carry):
            to = lax.rem(d + k, N_DP)
            rcopy(
                send.at[which, to], got.at[which, d],
                route_ss.at[which, k], route_rs.at[which, k], at(to, f),
            ).wait_send()
            return carry

        lax.fori_loop(1, N_DP, step, 0)

    route(0)

    xr, xl, xo = lax.rem(x + 1, NX), lax.rem(x + NX - 1, NX), lax.rem(x + 2, NX)
    x_order = ((1, xr), (3, xl), (2, xo))
    half = pl.ds(pl.multiple_of(192 * c, 192), 192)
    other_half = pl.ds(pl.multiple_of(192 - 192 * c, 192), 192)
    for k, to in x_order:
        go(
            prompt_ref.at[to, half],
            columns_in.at[k, half],
            x_ss.at[0, k], x_rs.at[0, k], at(to * NZ + z, f),
        )

    loads[6].wait()
    pad8 = jnp.zeros((CH, 8), BF16)
    for o in range(N_DP):
        lines = [weight_ref[k, :, TAPC * o : TAPC * o + TAPC] for k in (2, 1, 0)]
        weight_t[:, 128 * o : 128 * o + 128] = jnp.concatenate(lines + [pad8], axis=1)

    lane = iota((1, TOK), 1)
    inside = jnp.ones((1, TOK), F32)
    start = jnp.int32(0)
    for k in range(6):
        inside = jnp.where(lane == start, 0.0, inside)
        start = start + clips_ref[0, k]
    pad_rows = jnp.zeros((8, TOK), F32)

    bias = bias_ref[...].astype(F32).reshape(1, CH)
    bias = jnp.sum(jnp.where(iota((CH, CH), 0) == iota((CH, CH), 1), bias, 0.0), axis=1, keepdims=True)
    preact_ref[...] = jnp.broadcast_to(bias, (CH, TOK))

    def preact_block(g):
        lines = [
            nn(frames_all[pl.ds(g, 1), :, 256 * b : 256 * b + 256][0], halving[...]) for b in range(3)
        ]
        odd = jnp.concatenate([part[:, :128] for part in lines], axis=1)
        even = jnp.concatenate([part[:, 128:] for part in lines], axis=1)
        early = pltpu.roll(odd, 1, 1) * inside
        blocks = []
        for q in range(4):
            rows = slice(TAPC * q, TAPC * q + TAPC)
            blocks += [odd[rows], even[rows], early[rows], pad_rows]
        block = jnp.concatenate(blocks, axis=0).astype(BF16)
        xbuf[pl.ds(4 * g, 4)] = block.reshape(4, 128, TOK)
        preact_ref[...] += nn(weight_t[:, pl.ds(pl.multiple_of(g * 512, 512), 512)], block)

    loads[0].wait()
    preact_block(f)
    frames_ag.relay()
    frames_ag.from_mate(0)
    preact_block(y * 2 + 1 - c)
    frames_ag.near()
    preact_block(yl * 2 + c)
    preact_block(yr * 2 + c)
    frames_ag.far()

    def weight_out(k, carry):
        to = lax.rem(f + k, N_FSDP)
        rcopy(
            weight_t.at[:, pl.ds(pl.multiple_of(to * 512, 512), 512)], weight_in.at[f],
            w_ss.at[k], w_rs.at[k], at(d, to),
        ).start()
        return carry

    lax.fori_loop(1, N_FSDP, weight_out, 0)
    weight_in[pl.ds(f, 1)] = weight_t[:, pl.ds(pl.multiple_of(f * 512, 512), 512)][None]

    preact_block(yo * 2 + c)

    routed(0)
    tags = got[0, :, CAP:, :].astype(F32)
    numbers = (tags[:, 6, :] - 1.0) * 16.0 + tags[:, 7, :]

    def token_of(rows, first, most):
        spot = iota((N_DP, rows, 128), 1)
        match = (iota((N_DP, rows, 128), 2) == spot + first) & (spot < most)
        picked = jnp.sum(jnp.where(match, numbers[:, None, :], 0.0), axis=2, keepdims=True)
        ok = iota((N_DP, rows, 1), 1) < most
        return jnp.where(ok, picked, -1.0)

    def token_hot(rows, first, most):
        token = iota((N_DP, rows, TOK), 2).astype(F32)
        return pick(token_of(rows, first, most) == token).reshape(N_DP * rows, TOK).astype(BF16)

    dlow[...] = token_hot(CAP, 0, CAP)
    for g in range(4):
        dhigh[g] = token_hot(8, 6 * g, 6)
    back_ref[...] = unpack(dlow, dhigh, got[0])

    for k, come in ((1, yl), (2, yr), (3, yo)):
        frames_ag.from_mate(k)
        preact_block(come * 2 + 1 - c)

    preact = preact_ref[...]
    cumul = 0.5 * (1.0 + lax.erf(preact * (1.0 / math.sqrt(2.0))))
    hidden_t = (preact * cumul).astype(BF16)
    send[1] = pack(dlow, dhigh, hidden_t)
    route(1)

    slope = cumul + preact * jnp.exp(-0.5 * preact * preact) * (1.0 / math.sqrt(2.0 * math.pi))
    slope_t = (back_ref[...] * slope).astype(BF16)
    slope_all[pl.ds(f, 1)] = slope_t[None]
    slope_ag = Gather(1, slope_all.at[f], slope_all)
    slope_ag.first()

    to_right, to_left = at(xr * NZ + z, f), at(xl * NZ + z, f)

    def halves(owner, h):
        return parts.at[owner, pl.ds(4 * h, 4), pl.ds(0, XROWS)]

    def rs_send(src, k, dev):
        go(src, rs_in.at[k], rs_ss.at[k], rs_rs.at[k], dev)

    def rs_wait(k):
        arrived(rs_in.at[k], rs_ss.at[k], rs_rs.at[k])

    def conv_part(owner, h):
        g = 2 * owner + h
        block = nt(slope_t, xbuf[pl.ds(4 * g, 4)].reshape(512, TOK))
        for q in range(4):
            parts[pl.ds(owner, 1), 4 * h + q] = block[:, 128 * q : 128 * q + 128].astype(BF16)[None]

    def rs_second():
        for k, owner, dev in ((0, xr, to_right), (1, xl, to_left)):
            rs_wait(k)
            total = halves(owner, k)[...].astype(F32) + rs_in[k].astype(F32)
            rs_out[k] = total.astype(BF16)
            rs_send(rs_out.at[k], 4 + k, dev)

    def rs_third():
        for k in (2, 3, 4, 5):
            rs_wait(k)
        for h, (one, two) in enumerate(((4, 3), (5, 2))):
            total = halves(x, h)[...].astype(F32) + rs_in[one].astype(F32)
            total = total + rs_in[two].astype(F32)
            conv_sum[pl.ds(4 * h, 4)] = total
            conv_send[pl.ds(4 * h, 4)] = total.astype(BF16)

    def z_at(offset):
        return lax.rem(z + NZ + offset, NZ)

    class ZSum:
        def __init__(self, which, chunk, value, dst, relay):
            self.ss, self.rs = z_ss.at[which], z_rs.at[which]
            self.chunk, self.value, self.dst, self.relayed = chunk, value, dst, relay

        def send(self, src, slot, to):
            go(src, self.dst.at[slot], self.ss.at[slot], self.rs.at[slot], at(x * NZ + z_at(to), f))

        def wait(self, slot):
            arrived(self.dst.at[slot], self.ss.at[slot], self.rs.at[slot])
            return self.dst[slot].astype(F32)

        def first(self):
            for slot, chunk, to in ((5, -4, -2), (6, -3, -1), (7, 3, 1), (1, 1, 1), (2, -1, -1)):
                self.send(self.chunk(z_at(chunk)), slot, to)

        def relay(self):
            total = self.value(z_at(-2)) + self.wait(5) + self.wait(6)
            self.relayed[0] = total.astype(BF16)
            self.send(self.relayed.at[0], 3, -2)
            self.relayed[1] = (self.value(z_at(2)) + self.wait(7)).astype(BF16)
            self.send(self.relayed.at[1], 4, 2)

        def total(self):
            total = self.value(z)
            for slot in (1, 2, 4, 3):
                total = total + self.wait(slot)
            return total

    z_conv = ZSum(
        0, lambda t: conv_send.at[t], lambda t: conv_sum[pl.ds(t, 1)][0], conv_got, conv_relay
    )
    z_parts = ZSum(
        1,
        lambda t: parts.at[:, t, pl.ds(XROWS, ZROWS)],
        lambda t: parts[:, pl.ds(t, 1), XROWS:, :][:, 0].astype(F32),
        parts_got,
        parts_relay,
    )
    z_adapter = ZSum(
        2, lambda t: adapter_send.at[t], lambda t: adapter_sum[pl.ds(t, 1)][0], adapter_got, adapter_relay
    )

    for k, (owner, h, dev) in enumerate(
        ((xo, 0, to_right), (xo, 1, to_left), (xr, 1, to_right), (xl, 0, to_left))
    ):
        conv_part(owner, h)
        rs_send(halves(owner, h), k, dev)
    conv_part(xr, 0)
    conv_part(xl, 1)
    conv_part(x, 0)
    conv_part(x, 1)

    for k, to in x_order:
        block = columns_in.at[k, half]
        arrived(block, x_ss.at[0, k], x_rs.at[0, k])
        go(block, block, x_ss.at[1, k], x_rs.at[1, k], mate)

    rs_second()

    routed(1)
    hidden_all[0] = unpack(slow, shigh, got[1]).astype(BF16)
    for k, to in x_order:
        go(hidden_all.at[0], hidden_all.at[k], x_ss.at[2, k], x_rs.at[2, k], at(to * NZ + z, f))
    z_parts.first()
    adapter_quarter[...] = nn(hidden_all[0], prompt_ref[pl.ds(x, 1)][0])
    slope_ag.relay()
    slope_ag.near()
    for k, to in x_order:
        arrived(columns_in.at[k, other_half], x_ss.at[1, k], x_rs.at[1, k])
    rs_third()
    z_conv.first()
    z_parts.relay()

    for k, to in x_order[:2]:
        arrived(hidden_all.at[k], x_ss.at[2, k], x_rs.at[2, k])
        adapter_quarter[...] += nn(hidden_all[k], columns_in[k])
    k = x_order[2][0]
    arrived(hidden_all.at[k], x_ss.at[2, k], x_rs.at[2, k])
    quarter = adapter_quarter[...] + nn(hidden_all[k], columns_in[k])
    for q in range(NZ):
        chunk = quarter[:, ECOL * q : ECOL * q + ECOL]
        chunk = jnp.concatenate([chunk, jnp.zeros((CH, 128 - ECOL), F32)], axis=1)
        adapter_sum[q] = chunk
        adapter_send[q] = chunk.astype(BF16)
    z_adapter.first()
    z_conv.relay()
    lines = z_parts.total()
    parts_sum[...] = lines
    parts_send[...] = lines.astype(BF16)
    for k, to in x_order:
        go(parts_send.at[to], parts_last.at[k], x_ss.at[3, k], x_rs.at[3, k], at(to * NZ + z, f))

    def weight_come(k, carry):
        come = lax.rem(f + N_FSDP - k, N_FSDP)
        rcopy(
            weight_in.at[come], weight_in.at[come], w_ss.at[k], w_rs.at[k], at(d, come)
        ).wait_recv()
        return carry

    lax.fori_loop(1, N_FSDP, weight_come, 0)
    for g in range(N_FSDP):
        weight_own[:, CH * g : CH * g + CH] = weight_in[g].T
    z_adapter.relay()
    slope_ag.far()
    for k in range(4):
        slope_ag.from_mate(k)
    grads = nn(weight_own[...], slope_all[...].reshape(N_FSDP * CH, TOK))
    odd, even = [], []
    for q in range(4):
        lines = grads[128 * q : 128 * q + 128]
        odd.append(lines[:TAPC] + pltpu.roll(lines[2 * TAPC : 3 * TAPC] * inside, TOK - 1, 1))
        even.append(lines[TAPC : 2 * TAPC])
    odd = jnp.concatenate(odd, axis=0).astype(BF16)
    even = jnp.concatenate(even, axis=0).astype(BF16)
    for b in range(3):
        both = jnp.concatenate(
            [odd[:, 128 * b : 128 * b + 128], even[:, 128 * b : 128 * b + 128]], axis=1
        )
        hidden_ref[:, 256 * b : 256 * b + 256] = nt(both, halving[...]).astype(BF16)

    sums_ref[0, :XROWS] = z_conv.total() * GRAD_SCALE
    total = parts_sum[pl.ds(x, 1)][0]
    for k, to in x_order:
        arrived(parts_last.at[k], x_ss.at[3, k], x_rs.at[3, k])
        total = total + parts_last[k].astype(F32)
    sums_ref[0, XROWS:] = total * GRAD_SCALE
    sums_ref[1] = z_adapter.total() * GRAD_SCALE

    for copy in pending:
        copy.wait_send()
    route_sent(0)
    route_sent(1)

    def weight_sent(k, carry):
        to = lax.rem(f + k, N_FSDP)
        rcopy(
            weight_t.at[:, pl.ds(pl.multiple_of(to * 512, 512), 512)], weight_in.at[f],
            w_ss.at[k], w_rs.at[k], at(d, to),
        ).wait_send()
        return carry

    lax.fori_loop(1, N_FSDP, weight_sent, 0)


def finish(hidden_in, sums_ref, hidden_ref, gadapter_ref, gconv_ref):
    hidden_ref[...] = hidden_in[...]
    conv = sums_ref[0].T
    gconv_ref[0] = conv[2 * TAPC : 3 * TAPC]
    gconv_ref[1] = conv[TAPC : 2 * TAPC]
    gconv_ref[2] = conv[:TAPC]
    gadapter_ref[...] = sums_ref[1][:, :ECOL]


def body(
    hidden_frames, conv_weight, conv_bias, adapter_weight, prompt_grad, token_index, clip_tokens
):
    vmem = pl.BlockSpec(memory_space=pltpu.VMEM)
    smem = pl.BlockSpec(memory_space=pltpu.SMEM)
    hbm = pl.BlockSpec(memory_space=pl.ANY)
    dma = pltpu.SemaphoreType.DMA
    hidden, sums = pl.pallas_call(
        kernel,
        out_shape=(
            jax.ShapeDtypeStruct((CH, 2 * TOK), BF16),
            jax.ShapeDtypeStruct((2, CH, 128), F32),
        ),
        in_specs=[hbm, hbm, vmem, hbm, hbm, vmem, smem],
        out_specs=(vmem, vmem),
        scratch_shapes=[
            pltpu.VMEM((N_FSDP, CH, 2 * TOK), BF16),
            pltpu.VMEM((3, CH, N_FSDP * CH), BF16),
            pltpu.VMEM((CH, WIDTH), BF16),
            pltpu.VMEM((NX, TOK, QUARTER), BF16),
            dma((7,)),
            pltpu.VMEM((256, 256), BF16),
            pltpu.VMEM((CH, TOK), F32),
            pltpu.VMEM((CH, TOK), F32),
            pltpu.VMEM((CH, N_DP * 128), BF16),
            pltpu.VMEM((N_FSDP, CH, 512), BF16),
            pltpu.VMEM((512, N_FSDP * CH), BF16),
            pltpu.VMEM((N_DP, 128, TOK), BF16),
            pltpu.VMEM((N_DP * CAP, TOK), BF16),
            pltpu.VMEM((4, N_DP * 8, TOK), BF16),
            pltpu.VMEM((N_DP * CAP, TOK), BF16),
            pltpu.VMEM((4, N_DP * 8, TOK), BF16),
            pltpu.VMEM((2, N_DP, 32, 128), BF16),
            pltpu.VMEM((2, N_DP, 32, 128), BF16),
            pltpu.VMEM((N_FSDP, CH, TOK), BF16),
            pltpu.VMEM((NX, TOK, QUARTER), BF16),
            pltpu.VMEM((NX, CH, TOK), BF16),
            pltpu.VMEM((CH, QUARTER), F32),
            pltpu.VMEM((NZ, CH, 128), F32),
            pltpu.VMEM((NX, NZ, CH, 128), BF16),
            pltpu.VMEM((6, 4, XROWS, 128), BF16),
            pltpu.VMEM((2, 4, XROWS, 128), BF16),
            pltpu.VMEM((NZ, XROWS, 128), F32),
            pltpu.VMEM((NZ, XROWS, 128), BF16),
            pltpu.VMEM((NZ, XROWS, 128), BF16),
            pltpu.VMEM((2, XROWS, 128), BF16),
            pltpu.VMEM((NZ, NX, ZROWS, 128), BF16),
            pltpu.VMEM((2, NX, ZROWS, 128), BF16),
            pltpu.VMEM((NX, ZROWS, 128), F32),
            pltpu.VMEM((NX, ZROWS, 128), BF16),
            pltpu.VMEM((NX, ZROWS, 128), BF16),
            pltpu.VMEM((NZ, CH, 128), BF16),
            pltpu.VMEM((NZ, CH, 128), BF16),
            pltpu.VMEM((2, CH, 128), BF16),
            dma((2, N_DP)), dma((2, N_DP)),
            dma((2, 11)), dma((2, 11)),
            dma((N_FSDP,)), dma((N_FSDP,)),
            dma((6,)), dma((6,)),
            dma((3, NZ)), dma((3, NZ)),
            dma((4, NX)), dma((4, NX)),
        ],
        compiler_params=pltpu.CompilerParams(
            collective_id=0, has_side_effects=True, vmem_limit_bytes=56 * 1024 * 1024
        ),
    )(
        hidden_frames.T,
        jnp.swapaxes(conv_weight, 1, 2),
        conv_bias,
        adapter_weight,
        prompt_grad,
        token_index,
        clip_tokens,
    )
    hidden, gadapter, gconv = pl.pallas_call(
        finish,
        out_shape=(
            jax.ShapeDtypeStruct((CH, 2 * TOK), BF16),
            jax.ShapeDtypeStruct((CH, ECOL), F32),
            jax.ShapeDtypeStruct((3, TAPC, CH), F32),
        ),
        in_specs=[vmem, vmem],
        out_specs=(vmem, vmem, vmem),
    )(hidden, sums)
    return (hidden.T, gadapter, gconv)


def solution(mesh):
    placed = (
        P("dp", "fsdp"),
        P(None, None, "fsdp"),
        P("fsdp"),
        P("fsdp", None),
        P("dp", None),
        P("dp"),
        P("dp", None),
    )
    return jax.shard_map(
        body,
        mesh=mesh,
        in_specs=placed,
        out_specs=(P("dp", "fsdp"), P("fsdp", "dp"), P(None, "dp", "fsdp")),
        check_vma=False,
    )
```
